32 devices in a mesh: blk: 8 (over z, y), inner: 4 (over x, core).
Axes of the slice: x: 2, y: 2, z: 4, core: 2. Of those that a mesh axis runs over, the one named last changes fastest.
Arguments:
- query_emb: bfloat16 [320, 1536], P(('blk', 'inner')), may hold values from -2 to 2, as said below
- doc_emb: bfloat16 [320, 1536], P(('blk', 'inner')), may hold values from -2 to 2, as said below
- positive: int32 [320], P(('blk', 'inner')), may hold values from 0 to 319, each once
- query_source: int32 [320], P(('blk', 'inner')), may hold values from 0 to 39
- doc_source: int32 [320], P(('blk', 'inner')), may hold values from 0 to 39
Outputs:
- row_loss: float32 [320], P(('blk', 'inner'))
- grad_query: float32 [320, 1536], P(('blk', 'inner'))
- grad_doc: float32 [320, 1536], P(('blk', 'inner'))
The draws below stay inside these ranges and needn't reach their ends.
Inputs may be any that keep to these rules, and one draw needn't show every extreme that they name: `query_emb`: real embeddings of order 1536 ** -0.5 per entry. `doc_emb`: real embeddings of order 1536 ** -0.5 per entry.
All inputs are finite; a program needn't handle non-finite values.
Results may differ from the reference program's by a relative error of at most 0.005.
Values may be sent and summed in bfloat16 or wider, within the bound.
A program may use at most 64 MiB of HBM per device.

```python
import math
import jax
import jax.numpy as jnp
from jax import lax

D = 1536
PAIRS = 320


def shared_base(key):
    return jax.random.normal(key, (PAIRS, D), jnp.float32)


def draw_doc_emb(key, part):
    base = shared_base(key)
    return jnp.clip(base * D ** (-0.5), -2.0, 2.0).astype(jnp.bfloat16)


def draw_query_emb(key, part):
    key = jax.random.fold_in(key, 23)
    fresh = jax.random.normal(key, (PAIRS, D), jnp.float32)
    return jnp.clip(fresh * D ** (-0.5), -2.0, 2.0).astype(jnp.bfloat16)


def touch_ends(drawn, own_key, least, largest):
    index_at = [jax.random.randint(jax.random.fold_in(own_key, axis), (), 0, length) for axis, length in enumerate(drawn.shape)]
    widest = drawn.shape.index(max(drawn.shape))
    neighbour = index_at[:widest] + [(index_at[widest] + 1) % drawn.shape[widest]] + index_at[widest + 1:]
    return drawn.at[tuple(index_at)].set(least).at[tuple(neighbour)].set(largest)


def setup_inputs(seed: int = 0) -> dict:
    keys = jax.random.split(jax.random.key(seed), 6)
    query_emb = draw_query_emb(jax.random.fold_in(keys[5], 71), 0)
    doc_emb = draw_doc_emb(jax.random.fold_in(keys[5], 71), 0)
    positive = jax.random.permutation(keys[2], PAIRS).astype(jnp.int32)
    query_source = touch_ends(jax.random.randint(keys[3], (PAIRS,), 0, PAIRS // 8), jax.random.fold_in(keys[3], 1), 0, (PAIRS // 8) - 1).astype(jnp.int32)
    doc_source = touch_ends(jax.random.randint(keys[4], (PAIRS,), 0, PAIRS // 8), jax.random.fold_in(keys[4], 1), 0, (PAIRS // 8) - 1).astype(jnp.int32)
    return dict(query_emb=query_emb, doc_emb=doc_emb, positive=positive, query_source=query_source, doc_source=doc_source)


EPS = 1e-06
INV_TAU = 100.0
NEG = -1e+30

def unit_rows(values):
    widened = values.astype(jnp.float32)
    lengths = jnp.sqrt(lax.optimization_barrier(jnp.sum(widened * widened, axis=1, keepdims=True)) + EPS)
    return (widened / lengths, lengths)

def scaled_gram(left_rows, right_rows):
    return jnp.dot(left_rows, right_rows.T, preferred_element_type=jnp.float32) * INV_TAU

def pair_masks(row_info, col_info):
    row_qsource, row_dsource, row_target, row_global = row_info
    col_qsource, col_dsource, col_target, col_global = col_info
    mask_qd = (col_global[None, :] == row_target[:, None]) | (col_dsource[None, :] != row_qsource[:, None])
    mask_dq = (col_target[None, :] != row_global[:, None]) & (col_qsource[None, :] != row_dsource[:, None])
    mask_qq = col_qsource[None, :] != row_qsource[:, None]
    mask_dd = col_dsource[None, :] != row_dsource[:, None]
    twin_dq = (row_target[:, None] != col_global[None, :]) & (row_qsource[:, None] != col_dsource[None, :])
    twin_qd = (row_global[:, None] == col_target[None, :]) | (row_dsource[:, None] != col_qsource[None, :])
    return (mask_qd, mask_dq, mask_qq, mask_dd, twin_dq, twin_qd)

def masked_lse(scores_list, masks_list):
    peak = lax.optimization_barrier(jnp.max(jnp.where(masks_list[0], scores_list[0], NEG), axis=1))
    for scores, masked in zip(scores_list[1:], masks_list[1:]):
        peak = jnp.maximum(peak, lax.optimization_barrier(jnp.max(jnp.where(masked, scores, NEG), axis=1)))
    totals = jnp.zeros(peak.shape, jnp.float32)
    for scores, masked in zip(scores_list, masks_list):
        totals = totals + lax.optimization_barrier(jnp.sum(jnp.exp(jnp.where(masked, scores - peak[:, None], NEG)), axis=1))
    return peak + jnp.log(totals)

def weight(masked, scores, norms):
    return jnp.exp(jnp.where(masked, scores - norms, NEG))

def rounded(values):
    return lax.optimization_barrier(values.astype(jnp.bfloat16)).astype(jnp.float32)

def reference(query_emb, doc_emb, positive, query_source, doc_source):
    unit_query, query_len = unit_rows(query_emb)
    unit_doc, doc_len = unit_rows(doc_emb)
    query_wide = rounded(unit_query)
    doc_wide = rounded(unit_doc)
    pairs = query_emb.shape[0]
    every = jnp.arange(pairs, dtype=jnp.int32)
    size = math.gcd(pairs, 512)
    blocks = jnp.arange(pairs // size, dtype=jnp.int32)
    col_info = (query_source, doc_source, positive, every)

    def block_parts(block):
        first = (block * size).astype(jnp.int32)
        row_query = lax.dynamic_slice_in_dim(query_wide, first, size, 0)
        row_doc = lax.dynamic_slice_in_dim(doc_wide, first, size, 0)
        row_info = (lax.dynamic_slice_in_dim(query_source, first, size, 0), lax.dynamic_slice_in_dim(doc_source, first, size, 0), lax.dynamic_slice_in_dim(positive, first, size, 0), first + jnp.arange(size, dtype=jnp.int32))
        scores = (scaled_gram(row_query, doc_wide), scaled_gram(row_doc, query_wide), scaled_gram(row_query, query_wide), scaled_gram(row_doc, doc_wide))
        return (first, row_info, scores, pair_masks(row_info, col_info))

    def forward_block(block):
        first, row_info, scores, masks = block_parts(block)
        query_lse = masked_lse([scores[0], scores[2]], [masks[0], masks[2]])
        doc_lse = masked_lse([scores[1], scores[3]], [masks[1], masks[3]])
        hit = lax.optimization_barrier(jnp.sum(jnp.where(every[None, :] == row_info[2][:, None], scores[0], 0.0), axis=1))
        return (query_lse, doc_lse, hit)
    query_lse, doc_lse, hit = lax.map(forward_block, blocks)
    query_lse = query_lse.reshape(-1)
    doc_lse = doc_lse.reshape(-1)
    hit = hit.reshape(-1)
    norm_all = jnp.logaddexp(query_lse, jnp.take(doc_lse, positive))
    row_loss = norm_all - hit
    inverse = jnp.zeros((pairs,), jnp.int32).at[positive].set(every)
    doc_norm_all = jnp.take(norm_all, inverse)

    def backward_block(block):
        first, row_info, scores, masks = block_parts(block)
        row_norm = lax.dynamic_slice_in_dim(norm_all, first, size, 0)[:, None]
        row_doc_norm = lax.dynamic_slice_in_dim(doc_norm_all, first, size, 0)[:, None]
        qd_weight = weight(masks[0], scores[0], row_norm) + weight(masks[4], scores[0], doc_norm_all[None, :]) - (every[None, :] == row_info[2][:, None]).astype(jnp.float32)
        qq_weight = weight(masks[2], scores[2], row_norm) + weight(masks[2], scores[2], norm_all[None, :])
        dq_weight = weight(masks[1], scores[1], row_doc_norm) + weight(masks[5], scores[1], norm_all[None, :]) - (positive[None, :] == row_info[3][:, None]).astype(jnp.float32)
        dd_weight = weight(masks[3], scores[3], row_doc_norm) + weight(masks[3], scores[3], doc_norm_all[None, :])
        query_grad = (jnp.dot(rounded(qd_weight), doc_wide, preferred_element_type=jnp.float32) + jnp.dot(rounded(qq_weight), query_wide, preferred_element_type=jnp.float32)) * INV_TAU
        doc_grad = (jnp.dot(rounded(dq_weight), query_wide, preferred_element_type=jnp.float32) + jnp.dot(rounded(dd_weight), doc_wide, preferred_element_type=jnp.float32)) * INV_TAU
        return (query_grad, doc_grad)
    query_part, doc_part = lax.map(backward_block, blocks)
    query_part = query_part.reshape(pairs, -1)
    doc_part = doc_part.reshape(pairs, -1)
    grad_query = (query_part - unit_query * lax.optimization_barrier(jnp.sum(unit_query * query_part, axis=1, keepdims=True))) / query_len
    grad_doc = (doc_part - unit_doc * lax.optimization_barrier(jnp.sum(unit_doc * doc_part, axis=1, keepdims=True))) / doc_len
    return (row_loss, grad_query, grad_doc)
```

```python
import functools

import jax
import jax.numpy as jnp
from jax import lax
from jax.experimental import pallas as pl
from jax.experimental.pallas import tpu as pltpu
from jax.sharding import PartitionSpec as P

EPS = 1e-06
INV_TAU = 100.0
NEG = -1e30


def joined_2(value, axis, join):
    pieces = jax.tree.map(lambda part: lax.all_gather(part, axis), value)
    head = jax.tree.map(lambda part: part[0], pieces)
    tail = jax.tree.map(lambda part: part[1:], pieces)
    so_far, _ = lax.scan(lambda so_far, piece: (join(so_far, piece), None), head, tail)
    return so_far


def unit_rows(values):
    widened = values.astype(jnp.float32)
    lengths = jnp.sqrt(jnp.sum(widened * widened, axis=1, keepdims=True) + EPS)
    return (widened / lengths, lengths)


def scaled_gram(left_rows, right_rows):
    return (
        lax.dot_general(
            left_rows, right_rows, (((1,), (1,)), ((), ())), preferred_element_type=jnp.float32
        )
        * INV_TAU
    )


def pair_masks(row_info, col_info):
    row_qsource, row_dsource, row_target, row_global = row_info
    col_qsource, col_dsource, col_target, col_global = col_info
    mask_qd = (col_global[None, :] == row_target[:, None]) | (
        col_dsource[None, :] != row_qsource[:, None]
    )
    mask_dq = (col_target[None, :] != row_global[:, None]) & (
        col_qsource[None, :] != row_dsource[:, None]
    )
    mask_qq = col_qsource[None, :] != row_qsource[:, None]
    mask_dd = col_dsource[None, :] != row_dsource[:, None]
    twin_dq = (row_target[:, None] != col_global[None, :]) & (
        row_qsource[:, None] != col_dsource[None, :]
    )
    twin_qd = (row_global[:, None] == col_target[None, :]) | (
        row_dsource[:, None] != col_qsource[None, :]
    )
    return (mask_qd, mask_dq, mask_qq, mask_dd, twin_dq, twin_qd)


def masked_terms(scores_list, masks_list):
    peak = jnp.max(jnp.where(masks_list[0], scores_list[0], NEG), axis=1)
    for scores, masked in zip(scores_list[1:], masks_list[1:]):
        peak = jnp.maximum(peak, jnp.max(jnp.where(masked, scores, NEG), axis=1))
    totals = jnp.zeros(peak.shape, jnp.float32)
    for scores, masked in zip(scores_list, masks_list):
        totals = totals + jnp.sum(jnp.exp(jnp.where(masked, scores - peak[:, None], NEG)), axis=1)
    return (peak, totals)


def joined(former, latter):
    peak = jnp.maximum(former[0], latter[0])
    return (peak, former[1] * jnp.exp(former[0] - peak) + latter[1] * jnp.exp(latter[0] - peak))


def merge_stats(former, latter):
    query_pair = joined((former[0], former[1]), (latter[0], latter[1]))
    doc_pair = joined((former[2], former[3]), (latter[2], latter[3]))
    return (query_pair[0], query_pair[1], doc_pair[0], doc_pair[1], former[4] + latter[4])


def column_global(offset, amount, rows_dev, inner_count, inner_pos):
    flat = offset + jnp.arange(amount, dtype=jnp.int32)
    return flat // rows_dev * (inner_count * rows_dev) + inner_pos * rows_dev + flat % rows_dev


def weight(masked, scores, norms):
    return jnp.exp(jnp.where(masked, scores - norms, NEG))


def weighted(weights, right_rows):
    return jnp.dot(weights.astype(jnp.bfloat16), right_rows, preferred_element_type=jnp.float32)


def shards(query_emb, doc_emb, positive, query_source, doc_source):
    rows_dev = query_emb.shape[0]
    inner_count = lax.axis_size("inner")
    inner_pos = lax.axis_index("inner")
    blk_pos = lax.axis_index("blk")
    group_base = blk_pos * inner_count * rows_dev
    unit_query, query_len = unit_rows(query_emb)
    unit_doc, doc_len = unit_rows(doc_emb)
    query_half = unit_query.astype(jnp.bfloat16)
    doc_half = unit_doc.astype(jnp.bfloat16)
    row_query, row_doc, row_qsource, row_dsource, row_target = (
        lax.all_gather(query_half, "inner", axis=0, tiled=True),
        lax.all_gather(doc_half, "inner", axis=0, tiled=True),
        lax.all_gather(query_source, "inner", axis=0, tiled=True),
        lax.all_gather(doc_source, "inner", axis=0, tiled=True),
        lax.all_gather(positive, "inner", axis=0, tiled=True),
    )
    row_global = group_base + jnp.arange(row_query.shape[0], dtype=jnp.int32)
    own_start = inner_pos * rows_dev

    def col_index(offset, amount):
        return column_global(offset, amount, rows_dev, inner_count, inner_pos)

    row_count = row_query.shape[0]
    row_info = (row_qsource, row_dsource, row_target, row_global)

    def tile(pieces, offset):
        col_query, col_doc, col_qsource, col_dsource, col_target = pieces
        col_global = col_index(offset, col_query.shape[0])
        scores = (
            scaled_gram(row_query, col_doc),
            scaled_gram(row_doc, col_query),
            scaled_gram(row_query, col_query),
            scaled_gram(row_doc, col_doc),
        )
        masks = pair_masks(row_info, (col_qsource, col_dsource, col_target, col_global))
        return (col_global, scores, masks)

    empty_peak = jnp.full((row_count,), NEG, jnp.float32)
    empty_sum = jnp.zeros((row_count,), jnp.float32)
    start_stats = (empty_peak, empty_sum, empty_peak, empty_sum, empty_sum)
    columns = (
        lax.all_gather(query_half, "blk", axis=0, tiled=True),
        lax.all_gather(doc_half, "blk", axis=0, tiled=True),
        lax.all_gather(query_source, "blk", axis=0, tiled=True),
        lax.all_gather(doc_source, "blk", axis=0, tiled=True),
        lax.all_gather(positive, "blk", axis=0, tiled=True),
    )
    col_global, scores, masks = tile(columns, 0)
    query_side = masked_terms([scores[0], scores[2]], [masks[0], masks[2]])
    doc_side = masked_terms([scores[1], scores[3]], [masks[1], masks[3]])
    hit = jnp.sum(jnp.where(col_global[None, :] == row_target[:, None], scores[0], 0.0), axis=1)
    stats = merge_stats(start_stats, (query_side[0], query_side[1], doc_side[0], doc_side[1], hit))
    stats = joined_2(stats, "inner", merge_stats)
    query_lse = stats[0] + jnp.log(stats[1])
    doc_lse = stats[2] + jnp.log(stats[3])
    own_doc_lse = lax.dynamic_slice_in_dim(doc_lse, own_start, rows_dev, 0)
    doc_lse_all, target_all = (
        lax.all_gather(own_doc_lse, ("blk", "inner"), axis=0, tiled=True),
        lax.all_gather(positive, ("blk", "inner"), axis=0, tiled=True),
    )
    own_query_lse = lax.dynamic_slice_in_dim(query_lse, own_start, rows_dev, 0)
    own_hit = lax.dynamic_slice_in_dim(stats[4], own_start, rows_dev, 0)
    own_norm = jnp.logaddexp(own_query_lse, jnp.take(doc_lse_all, positive))
    row_loss = own_norm - own_hit
    norm_all = lax.all_gather(own_norm, ("blk", "inner"), axis=0, tiled=True)
    pairs = norm_all.shape[0]
    inverse = jnp.zeros((pairs,), jnp.int32).at[target_all].set(jnp.arange(pairs, dtype=jnp.int32))
    doc_norm_all = jnp.take(norm_all, inverse)
    row_norm = jnp.take(norm_all, row_global)[:, None]
    row_doc_norm = jnp.take(doc_norm_all, row_global)[:, None]
    col_global, scores, masks = tile(columns, 0)
    col_query = columns[0]
    col_doc = columns[1]
    col_target = columns[4]
    col_norm = jnp.take(norm_all, col_global)[None, :]
    col_doc_norm = jnp.take(doc_norm_all, col_global)[None, :]
    qd_weight = (
        weight(masks[0], scores[0], row_norm)
        + weight(masks[4], scores[0], col_doc_norm)
        - (col_global[None, :] == row_target[:, None]).astype(jnp.float32)
    )
    qq_weight = weight(masks[2], scores[2], row_norm) + weight(masks[2], scores[2], col_norm)
    dq_weight = (
        weight(masks[1], scores[1], row_doc_norm)
        + weight(masks[5], scores[1], col_norm)
        - (col_target[None, :] == row_global[:, None]).astype(jnp.float32)
    )
    dd_weight = weight(masks[3], scores[3], row_doc_norm) + weight(
        masks[3], scores[3], col_doc_norm
    )
    query_grad = (weighted(qd_weight, col_doc) + weighted(qq_weight, col_query)) * INV_TAU
    doc_grad = (weighted(dq_weight, col_query) + weighted(dd_weight, col_doc)) * INV_TAU
    query_part, doc_part = (
        lax.psum_scatter(query_grad, "inner", scatter_dimension=0, tiled=True),
        lax.psum_scatter(doc_grad, "inner", scatter_dimension=0, tiled=True),
    )
    grad_query = (
        query_part - unit_query * jnp.sum(unit_query * query_part, axis=1, keepdims=True)
    ) / query_len
    grad_doc = (doc_part - unit_doc * jnp.sum(unit_doc * doc_part, axis=1, keepdims=True)) / doc_len
    return (row_loss, grad_query, grad_doc)


def gather_kernel(
    depth, q_ref, d_ref, pos_ref, qs_ref, ds_ref, loss_ref, gq_ref, gd_ref,
    buf, rows_all, unit_own, len_own, scol, ucol, srow, urow, lse_self, lse_pair, send_sem, recv_sem,
):
    f32, bf16 = jnp.float32, jnp.bfloat16
    rows = q_ref.shape[0]
    width = q_ref.shape[1]
    quarter = width // 4
    blk, inner = lax.axis_index("blk"), lax.axis_index("inner")
    z, y = blk // 2, blk % 2
    x, core = inner // 2, inner % 2
    me = blk * 4 + inner

    def place(zz, flip_a, flip_b):
        flip_y = flip_a * (1 - core) + flip_b * core
        flip_x = flip_a * core + flip_b * (1 - core)
        yy = y + flip_y * (1 - 2 * y)
        xx = x + flip_x * (1 - 2 * x)
        return zz * 2 + yy, xx * 2 + core

    def slot_of(zz, flip_a, flip_b):
        b, i = place(zz, flip_a, flip_b)
        return b * 4 + i

    peer_a = place(z, 1, 0)
    peer_b = place(z, 0, 1)
    peer_core = (blk, x * 2 + 1 - core)
    peer_up = (blk + 2, inner)
    peer_down = (blk - 2, inner)

    barrier = pltpu.get_barrier_semaphore()

    def greet(peer):
        pl.semaphore_signal(barrier, inc=1, device_id=peer, device_id_type=pl.DeviceIdType.MESH)

    greet(peer_a)
    greet(peer_b)
    greet(peer_core)

    @pl.when(z < depth - 1)
    def _():
        greet(peer_up)

    @pl.when(z > 0)
    def _():
        greet(peer_down)

    unit_own[...] = jnp.zeros_like(unit_own)
    len_own[...] = jnp.ones_like(len_own)
    for ref, first in ((q_ref, 0), (d_ref, 16)):
        wide = ref[...].astype(f32)
        lengths = jnp.sqrt(jnp.sum(wide * wide, axis=1, keepdims=True) + EPS)
        unit_own[pl.ds(first, rows), :] = wide / lengths
        len_own[pl.ds(first, rows), :] = jnp.broadcast_to(lengths, (rows, 128))
    own = unit_own[...].astype(bf16)

    row = lax.broadcasted_iota(jnp.int32, (32, 128), 0)
    lane = lax.broadcasted_iota(jnp.int32, (32, 128), 1)
    source = jnp.zeros((32, 128), jnp.int32)
    key = jnp.zeros((32, 128), jnp.int32)
    for r in range(rows):
        source = jnp.where(row == r, qs_ref[r], source)
        source = jnp.where(row == 16 + r, ds_ref[r], source)
        key = jnp.where(row == r, pos_ref[r], key)
    key = jnp.where(row >= 16, me * rows + row - 16, key)
    kind = jnp.where(row >= 16, 0.25, 0.0).astype(f32)
    valid = (row % 16) < rows
    own_source = source.astype(f32)
    own_key = jnp.where(valid, key.astype(f32) + kind, -100.0)
    parts = (
        (source >> 5).astype(f32),
        (source & 31).astype(f32),
        (key >> 5).astype(f32),
        (key & 31).astype(f32) + kind,
    )

    def lanes(first):
        out = jnp.zeros((32, 128), f32)
        for k, part in enumerate(parts):
            out = jnp.where(lane == first + k, part, out)
        return out.astype(bf16)

    def select(shape, chosen):
        r = lax.broadcasted_iota(jnp.int32, shape, 0)
        c = lax.broadcasted_iota(jnp.int32, shape, 1)
        return chosen(r, c).astype(f32).astype(bf16)

    def mm(a, b):
        return jnp.dot(a, b, preferred_element_type=f32)

    def mmt(a, b):
        return lax.dot_general(a, b, (((1,), (1,)), ((), ())), preferred_element_type=f32)

    head = select((16, 32), lambda r, c: c == jnp.where(r < rows, r, r + 16 - rows))
    rest = [
        select((16, 32), lambda r, c, k=k: (r // 4 == k) & (c == 32 - rows + r % 4)) for k in range(4)
    ]
    mine = pl.ds(pl.multiple_of(me * 16, 16), 16)
    buf[mine, 0:width] = mm(head, own).astype(bf16)
    tail = mm(rest[0], own[:, 0:quarter])
    for k in range(1, 4):
        tail = tail + mm(rest[k], own[:, k * quarter : (k + 1) * quarter])
    buf[mine, width : width + quarter] = tail.astype(bf16)
    buf[mine, width + quarter :] = (mm(head, lanes(0)) + mm(rest[0], lanes(4))).astype(bf16)

    pl.semaphore_wait(barrier, 3 + jnp.minimum(z, 1) + jnp.minimum(depth - 1 - z, 1))

    def copy(slot, sem, peer):
        piece = buf.at[pl.ds(pl.multiple_of(slot * 16, 16), 16)]
        return pltpu.make_async_remote_copy(
            src_ref=piece, dst_ref=piece, send_sem=send_sem.at[sem], recv_sem=recv_sem.at[slot],
            device_id=peer, device_id_type=pl.DeviceIdType.MESH,
        )

    def sends(zz, flip_a, flip_b):
        slot = slot_of(zz, flip_a, flip_b)
        out = []
        if not flip_a and not flip_b:
            out.append((copy(slot, zz, peer_up), (zz <= z) & (z < depth - 1)))
            out.append((copy(slot, depth + zz, peer_down), (zz >= z) & (z > 0)))
            out.append((copy(slot, 2 * depth + zz, peer_a), None))
        if not flip_b:
            out.append((copy(slot, (3 + flip_a) * depth + zz, peer_b), None))
        out.append((copy(slot, (5 + 2 * flip_b + flip_a) * depth + zz, peer_core), None))
        return out

    def each(copies, act):
        for one, under in copies:
            if under is None:
                act(one)
            else:
                pl.when(under)(functools.partial(act, one))

    def start(one):
        one.start()

    def arrive(slot):
        copy(slot, 0, peer_core).wait_recv()

    def handle(dist, flip_a, flip_b):
        def at(zz):
            if dist or flip_a or flip_b:
                arrive(slot_of(zz, flip_a, flip_b))
            each(sends(zz, flip_a, flip_b), start)

        if dist == 0:
            at(z)
        else:
            pl.when(z - dist >= 0)(lambda: at(z - dist))
            pl.when(z + dist < depth)(lambda: at(z + dist))

    order = sorted(
        ((dist + a + b, a + b, dist, a, b) for dist in range(depth) for a in (0, 1) for b in (0, 1))
    )
    for _, _, dist, a, b in order:
        handle(dist, a, b)

    def from_core(zz, carry):
        for fb in (0, 1):
            for fa in (0, 1):
                s = slot_of(zz, fa, fb)
                arrive(s + 1 - 2 * core)
        return carry

    lax.fori_loop(0, depth, from_core, 0)

    count = 2 * rows * buf.shape[0] // 16
    heads = buf.shape[0]
    tails = count - heads
    rows_all[0:heads, :] = buf[:, 0:width]
    left = buf[:, width : width + quarter]
    meta = buf[:, width + quarter :]
    picks = [
        select((tails, heads), lambda r, c, k=k: c == r // 4 * 16 + k * 4 + r % 4) for k in range(4)
    ]
    for k in range(4):
        rows_all[heads:, k * quarter : (k + 1) * quarter] = mm(picks[k], left).astype(bf16)
    meta_tail = mm(picks[0], meta).astype(bf16)

    def reader(first, axis, shape):
        pos = lax.broadcasted_iota(jnp.int32, shape, axis)
        return jnp.where(pos == first, 32.0, jnp.where(pos == first + 1, 1.0, 0.0)).astype(bf16)

    for ref, first in ((scol, 0), (ucol, 2)):
        ref[0:heads, :] = mm(meta, reader(first, 0, (128, 128)))
        ref[heads:, :] = mm(meta_tail, reader(first + 4, 0, (128, 128)))
    for ref, first in ((srow, 0), (urow, 2)):
        ref[:, 0:heads] = mmt(reader(first, 1, (8, 128)), meta)
        ref[:, heads:] = mmt(reader(first + 4, 1, (8, 128)), meta_tail)
    s_row, u_row = srow[0:1, :], urow[0:1, :]
    lse_self[...] = jnp.zeros_like(lse_self)
    lse_pair[...] = jnp.zeros_like(lse_pair)
    chunk = 128

    def forward(step, carry):
        at = pl.ds(pl.multiple_of(step * chunk, chunk), chunk)
        scores = mmt(rows_all[at, :], rows_all[...]) * INV_TAU
        apart = u_row - ucol[at, 0:1]
        allowed = (apart == 0.25) | ((s_row != scol[at, 0:1]) & (apart != -0.25))
        scores = jnp.where(allowed, scores, NEG)
        peak = jnp.max(scores, axis=1, keepdims=True)
        total = jnp.sum(jnp.exp(scores - peak), axis=1, keepdims=True)
        lse = jnp.where(peak > 0.5 * NEG, peak + jnp.log(total), NEG)
        lse_self[0:1, :] += jnp.sum(jnp.where(apart == 0.0, lse, 0.0), axis=0, keepdims=True)
        lse_pair[0:1, :] += jnp.sum(
            jnp.where(jnp.abs(apart) == 0.25, lse, 0.0), axis=0, keepdims=True
        )
        return carry

    lax.fori_loop(0, count // chunk, forward, 0)
    first, second = lse_self[0:1, :], lse_pair[0:1, :]
    norm_row = jnp.maximum(first, second) + jnp.log(1.0 + jnp.exp(-jnp.abs(first - second)))

    scores = mmt(own, rows_all[...]) * INV_TAU
    apart = u_row - own_key[:, 0:1]
    hit = jnp.abs(apart) == 0.25
    norm_own = jnp.sum(jnp.where(apart == 0.0, norm_row, 0.0), axis=1, keepdims=True)
    loss = norm_own - jnp.sum(jnp.where(hit, scores, 0.0), axis=1, keepdims=True)
    loss_ref[...] = jnp.broadcast_to(loss, loss_ref.shape)
    from_own = jnp.exp(scores - norm_own)
    apart_source = (s_row != own_source[:, 0:1]) & (own_key[:, 0:1] >= 0.0)
    weights = jnp.where(
        hit, from_own - 1.0, jnp.where(apart_source, from_own + jnp.exp(scores - norm_row), 0.0)
    )
    grads = mm(weights.astype(bf16), rows_all[...]) * INV_TAU
    unit = unit_own[...]
    grads = (grads - unit * jnp.sum(unit * grads, axis=1, keepdims=True)) / len_own[:, 0:1]
    gq_ref[...] = grads[0:rows, :]
    gd_ref[...] = grads[16 : 16 + rows, :]

    def done(one):
        one.wait_send()

    def finish(zz, carry):
        for fa in (0, 1):
            for fb in (0, 1):
                each(sends(zz, fa, fb), done)
        return carry

    lax.fori_loop(0, depth, finish, 0)


def whole_batch(depth, query_emb, doc_emb, positive, query_source, doc_source):
    rows, width = query_emb.shape
    devices = lax.axis_size("blk") * lax.axis_size("inner")
    count = 2 * rows * devices
    vmem = pl.BlockSpec(memory_space=pltpu.VMEM)
    smem = pl.BlockSpec(memory_space=pltpu.SMEM)
    f32 = jnp.float32
    loss, grad_query, grad_doc = pl.pallas_call(
        functools.partial(gather_kernel, depth),
        out_shape=(
            jax.ShapeDtypeStruct((32, 128), f32),
            jax.ShapeDtypeStruct((rows, width), f32),
            jax.ShapeDtypeStruct((rows, width), f32),
        ),
        in_specs=[vmem, vmem, smem, smem, smem],
        out_specs=(vmem, vmem, vmem),
        scratch_shapes=[
            pltpu.VMEM((devices * 16, width + width // 4 + 128), jnp.bfloat16),
            pltpu.VMEM((count, width), jnp.bfloat16),
            pltpu.VMEM((32, width), f32),
            pltpu.VMEM((32, 128), f32),
            pltpu.VMEM((count, 128), f32),
            pltpu.VMEM((count, 128), f32),
            pltpu.VMEM((8, count), f32),
            pltpu.VMEM((8, count), f32),
            pltpu.VMEM((8, count), f32),
            pltpu.VMEM((8, count), f32),
            pltpu.SemaphoreType.DMA((9 * depth,)),
            pltpu.SemaphoreType.DMA((devices,)),
        ],
        compiler_params=pltpu.CompilerParams(
            collective_id=0, has_side_effects=True, vmem_limit_bytes=40 * 1024 * 1024
        ),
    )(query_emb, doc_emb, positive, query_source, doc_source)
    return (loss[:rows, 0], grad_query, grad_doc)


def solution(mesh):
    small = mesh.shape["inner"] == 4 and mesh.shape["blk"] == 8
    body = functools.partial(whole_batch, mesh.shape["blk"] // 2) if small else shards
    placed = (
        P(("blk", "inner"), None),
        P(("blk", "inner"), None),
        P(("blk", "inner")),
        P(("blk", "inner")),
        P(("blk", "inner")),
    )
    return jax.shard_map(
        body,
        mesh=mesh,
        in_specs=placed,
        out_specs=(P(("blk", "inner")), P(("blk", "inner"), None), P(("blk", "inner"), None)),
        check_vma=False,
    )
```

```python
import functools

import jax
import jax.numpy as jnp
from jax import lax
from jax.experimental import pallas as pl
from jax.experimental.pallas import tpu as pltpu
from jax.sharding import PartitionSpec as P

EPS = 1e-06
INV_TAU = 100.0
NEG = -1e30


def joined_2(value, axis, join):
    pieces = jax.tree.map(lambda part: lax.all_gather(part, axis), value)
    head = jax.tree.map(lambda part: part[0], pieces)
    tail = jax.tree.map(lambda part: part[1:], pieces)
    so_far, _ = lax.scan(lambda so_far, piece: (join(so_far, piece), None), head, tail)
    return so_far


def unit_rows(values):
    widened = values.astype(jnp.float32)
    lengths = jnp.sqrt(jnp.sum(widened * widened, axis=1, keepdims=True) + EPS)
    return (widened / lengths, lengths)


def scaled_gram(left_rows, right_rows):
    return (
        lax.dot_general(
            left_rows, right_rows, (((1,), (1,)), ((), ())), preferred_element_type=jnp.float32
        )
        * INV_TAU
    )


def pair_masks(row_info, col_info):
    row_qsource, row_dsource, row_target, row_global = row_info
    col_qsource, col_dsource, col_target, col_global = col_info
    mask_qd = (col_global[None, :] == row_target[:, None]) | (
        col_dsource[None, :] != row_qsource[:, None]
    )
    mask_dq = (col_target[None, :] != row_global[:, None]) & (
        col_qsource[None, :] != row_dsource[:, None]
    )
    mask_qq = col_qsource[None, :] != row_qsource[:, None]
    mask_dd = col_dsource[None, :] != row_dsource[:, None]
    twin_dq = (row_target[:, None] != col_global[None, :]) & (
        row_qsource[:, None] != col_dsource[None, :]
    )
    twin_qd = (row_global[:, None] == col_target[None, :]) | (
        row_dsource[:, None] != col_qsource[None, :]
    )
    return (mask_qd, mask_dq, mask_qq, mask_dd, twin_dq, twin_qd)


def masked_terms(scores_list, masks_list):
    peak = jnp.max(jnp.where(masks_list[0], scores_list[0], NEG), axis=1)
    for scores, masked in zip(scores_list[1:], masks_list[1:]):
        peak = jnp.maximum(peak, jnp.max(jnp.where(masked, scores, NEG), axis=1))
    totals = jnp.zeros(peak.shape, jnp.float32)
    for scores, masked in zip(scores_list, masks_list):
        totals = totals + jnp.sum(jnp.exp(jnp.where(masked, scores - peak[:, None], NEG)), axis=1)
    return (peak, totals)


def joined(former, latter):
    peak = jnp.maximum(former[0], latter[0])
    return (peak, former[1] * jnp.exp(former[0] - peak) + latter[1] * jnp.exp(latter[0] - peak))


def merge_stats(former, latter):
    query_pair = joined((former[0], former[1]), (latter[0], latter[1]))
    doc_pair = joined((former[2], former[3]), (latter[2], latter[3]))
    return (query_pair[0], query_pair[1], doc_pair[0], doc_pair[1], former[4] + latter[4])


def column_global(offset, amount, rows_dev, inner_count, inner_pos):
    flat = offset + jnp.arange(amount, dtype=jnp.int32)
    return flat // rows_dev * (inner_count * rows_dev) + inner_pos * rows_dev + flat % rows_dev


def weight(masked, scores, norms):
    return jnp.exp(jnp.where(masked, scores - norms, NEG))


def weighted(weights, right_rows):
    return jnp.dot(weights.astype(jnp.bfloat16), right_rows, preferred_element_type=jnp.float32)


def shards(query_emb, doc_emb, positive, query_source, doc_source):
    rows_dev = query_emb.shape[0]
    inner_count = lax.axis_size("inner")
    inner_pos = lax.axis_index("inner")
    blk_pos = lax.axis_index("blk")
    group_base = blk_pos * inner_count * rows_dev
    unit_query, query_len = unit_rows(query_emb)
    unit_doc, doc_len = unit_rows(doc_emb)
    query_half = unit_query.astype(jnp.bfloat16)
    doc_half = unit_doc.astype(jnp.bfloat16)
    row_query, row_doc, row_qsource, row_dsource, row_target = (
        lax.all_gather(query_half, "inner", axis=0, tiled=True),
        lax.all_gather(doc_half, "inner", axis=0, tiled=True),
        lax.all_gather(query_source, "inner", axis=0, tiled=True),
        lax.all_gather(doc_source, "inner", axis=0, tiled=True),
        lax.all_gather(positive, "inner", axis=0, tiled=True),
    )
    row_global = group_base + jnp.arange(row_query.shape[0], dtype=jnp.int32)
    own_start = inner_pos * rows_dev

    def col_index(offset, amount):
        return column_global(offset, amount, rows_dev, inner_count, inner_pos)

    row_count = row_query.shape[0]
    row_info = (row_qsource, row_dsource, row_target, row_global)

    def tile(pieces, offset):
        col_query, col_doc, col_qsource, col_dsource, col_target = pieces
        col_global = col_index(offset, col_query.shape[0])
        scores = (
            scaled_gram(row_query, col_doc),
            scaled_gram(row_doc, col_query),
            scaled_gram(row_query, col_query),
            scaled_gram(row_doc, col_doc),
        )
        masks = pair_masks(row_info, (col_qsource, col_dsource, col_target, col_global))
        return (col_global, scores, masks)

    empty_peak = jnp.full((row_count,), NEG, jnp.float32)
    empty_sum = jnp.zeros((row_count,), jnp.float32)
    start_stats = (empty_peak, empty_sum, empty_peak, empty_sum, empty_sum)
    columns = (
        lax.all_gather(query_half, "blk", axis=0, tiled=True),
        lax.all_gather(doc_half, "blk", axis=0, tiled=True),
        lax.all_gather(query_source, "blk", axis=0, tiled=True),
        lax.all_gather(doc_source, "blk", axis=0, tiled=True),
        lax.all_gather(positive, "blk", axis=0, tiled=True),
    )
    col_global, scores, masks = tile(columns, 0)
    query_side = masked_terms([scores[0], scores[2]], [masks[0], masks[2]])
    doc_side = masked_terms([scores[1], scores[3]], [masks[1], masks[3]])
    hit = jnp.sum(jnp.where(col_global[None, :] == row_target[:, None], scores[0], 0.0), axis=1)
    stats = merge_stats(start_stats, (query_side[0], query_side[1], doc_side[0], doc_side[1], hit))
    stats = joined_2(stats, "inner", merge_stats)
    query_lse = stats[0] + jnp.log(stats[1])
    doc_lse = stats[2] + jnp.log(stats[3])
    own_doc_lse = lax.dynamic_slice_in_dim(doc_lse, own_start, rows_dev, 0)
    doc_lse_all, target_all = (
        lax.all_gather(own_doc_lse, ("blk", "inner"), axis=0, tiled=True),
        lax.all_gather(positive, ("blk", "inner"), axis=0, tiled=True),
    )
    own_query_lse = lax.dynamic_slice_in_dim(query_lse, own_start, rows_dev, 0)
    own_hit = lax.dynamic_slice_in_dim(stats[4], own_start, rows_dev, 0)
    own_norm = jnp.logaddexp(own_query_lse, jnp.take(doc_lse_all, positive))
    row_loss = own_norm - own_hit
    norm_all = lax.all_gather(own_norm, ("blk", "inner"), axis=0, tiled=True)
    pairs = norm_all.shape[0]
    inverse = jnp.zeros((pairs,), jnp.int32).at[target_all].set(jnp.arange(pairs, dtype=jnp.int32))
    doc_norm_all = jnp.take(norm_all, inverse)
    row_norm = jnp.take(norm_all, row_global)[:, None]
    row_doc_norm = jnp.take(doc_norm_all, row_global)[:, None]
    col_global, scores, masks = tile(columns, 0)
    col_query = columns[0]
    col_doc = columns[1]
    col_target = columns[4]
    col_norm = jnp.take(norm_all, col_global)[None, :]
    col_doc_norm = jnp.take(doc_norm_all, col_global)[None, :]
    qd_weight = (
        weight(masks[0], scores[0], row_norm)
        + weight(masks[4], scores[0], col_doc_norm)
        - (col_global[None, :] == row_target[:, None]).astype(jnp.float32)
    )
    qq_weight = weight(masks[2], scores[2], row_norm) + weight(masks[2], scores[2], col_norm)
    dq_weight = (
        weight(masks[1], scores[1], row_doc_norm)
        + weight(masks[5], scores[1], col_norm)
        - (col_target[None, :] == row_global[:, None]).astype(jnp.float32)
    )
    dd_weight = weight(masks[3], scores[3], row_doc_norm) + weight(
        masks[3], scores[3], col_doc_norm
    )
    query_grad = (weighted(qd_weight, col_doc) + weighted(qq_weight, col_query)) * INV_TAU
    doc_grad = (weighted(dq_weight, col_query) + weighted(dd_weight, col_doc)) * INV_TAU
    query_part, doc_part = (
        lax.psum_scatter(query_grad, "inner", scatter_dimension=0, tiled=True),
        lax.psum_scatter(doc_grad, "inner", scatter_dimension=0, tiled=True),
    )
    grad_query = (
        query_part - unit_query * jnp.sum(unit_query * query_part, axis=1, keepdims=True)
    ) / query_len
    grad_doc = (doc_part - unit_doc * jnp.sum(unit_doc * doc_part, axis=1, keepdims=True)) / doc_len
    return (row_loss, grad_query, grad_doc)


def gather_kernel(
    depth, q_hbm, d_hbm, pos_hbm, qs_hbm, ds_hbm, loss_ref, gq_ref, gd_ref,
    q_ref, d_ref, pos_ref, qs_ref, ds_ref, in_sem, buf, rows_all, unit_own, len_own, scol, ucol, srow, urow, lse_self, lse_pair, send_sem, recv_sem,
):
    f32, bf16 = jnp.float32, jnp.bfloat16
    rows = q_ref.shape[0]
    width = q_ref.shape[1]
    quarter = width // 4
    blk, inner = lax.axis_index("blk"), lax.axis_index("inner")
    z, y = blk // 2, blk % 2
    x, core = inner // 2, inner % 2
    me = blk * 4 + inner

    def place(zz, flip_a, flip_b):
        flip_y = flip_a * (1 - core) + flip_b * core
        flip_x = flip_a * core + flip_b * (1 - core)
        yy = y + flip_y * (1 - 2 * y)
        xx = x + flip_x * (1 - 2 * x)
        return zz * 2 + yy, xx * 2 + core

    def slot_of(zz, flip_a, flip_b):
        b, i = place(zz, flip_a, flip_b)
        return b * 4 + i

    peer_a = place(z, 1, 0)
    peer_b = place(z, 0, 1)
    peer_diag = place(z, 1, 1)
    peer_core = (blk, x * 2 + 1 - core)
    upper = z // (depth // 2)
    low = z * (1 - upper) + (depth - 1 - z) * upper

    def near(k):
        kth = k + jnp.minimum(jnp.maximum(k - low + 1, 0), 1)
        return kth * (1 - upper) + (depth - 1 - kth) * upper

    line = [near(k) for k in range(depth - 1)]

    barrier = pltpu.get_barrier_semaphore()
    peers = [(zz * 2 + y, inner) for zz in line] + [peer_a, peer_b, peer_diag, peer_core]
    for peer in peers:
        pl.semaphore_signal(barrier, inc=1, device_id=peer, device_id_type=pl.DeviceIdType.MESH)

    held = ((q_hbm, q_ref), (d_hbm, d_ref), (pos_hbm, pos_ref), (qs_hbm, qs_ref), (ds_hbm, ds_ref))
    loads = [pltpu.make_async_copy(a, b, in_sem.at[n]) for n, (a, b) in enumerate(held)]
    for load in loads:
        load.start()
    for load in loads:
        load.wait()
    unit_own[...] = jnp.zeros_like(unit_own)
    len_own[...] = jnp.ones_like(len_own)
    for ref, first in ((q_ref, 0), (d_ref, 16)):
        wide = ref[...].astype(f32)
        lengths = jnp.sqrt(jnp.sum(wide * wide, axis=1, keepdims=True) + EPS)
        unit_own[pl.ds(first, rows), :] = wide / lengths
        len_own[pl.ds(first, rows), :] = jnp.broadcast_to(lengths, (rows, 128))
    own = unit_own[...].astype(bf16)

    row = lax.broadcasted_iota(jnp.int32, (32, 128), 0)
    lane = lax.broadcasted_iota(jnp.int32, (32, 128), 1)
    source = jnp.zeros((32, 128), jnp.int32)
    key = jnp.zeros((32, 128), jnp.int32)
    for r in range(rows):
        source = jnp.where(row == r, qs_ref[r], source)
        source = jnp.where(row == 16 + r, ds_ref[r], source)
        key = jnp.where(row == r, pos_ref[r], key)
    key = jnp.where(row >= 16, me * rows + row - 16, key)
    kind = jnp.where(row >= 16, 0.25, 0.0).astype(f32)
    valid = (row % 16) < rows
    own_source = source.astype(f32)
    own_key = jnp.where(valid, key.astype(f32) + kind, -100.0)
    parts = (
        (source >> 5).astype(f32),
        (source & 31).astype(f32),
        (key >> 5).astype(f32),
        (key & 31).astype(f32) + kind,
    )

    def lanes(first):
        out = jnp.zeros((32, 128), f32)
        for k, part in enumerate(parts):
            out = jnp.where(lane == first + k, part, out)
        return out.astype(bf16)

    def select(shape, chosen):
        r = lax.broadcasted_iota(jnp.int32, shape, 0)
        c = lax.broadcasted_iota(jnp.int32, shape, 1)
        return chosen(r, c).astype(f32).astype(bf16)

    def mm(a, b):
        return jnp.dot(a, b, preferred_element_type=f32)

    def mmt(a, b):
        return lax.dot_general(a, b, (((1,), (1,)), ((), ())), preferred_element_type=f32)

    head = select((16, 32), lambda r, c: c == jnp.where(r < rows, r, r + 16 - rows))
    rest = [
        select((16, 32), lambda r, c, k=k: (r // 4 == k) & (c == 32 - rows + r % 4)) for k in range(4)
    ]
    mine = pl.ds(pl.multiple_of(me * 16, 16), 16)
    buf[mine, 0:width] = mm(head, own).astype(bf16)
    tail = mm(rest[0], own[:, 0:quarter])
    for k in range(1, 4):
        tail = tail + mm(rest[k], own[:, k * quarter : (k + 1) * quarter])
    buf[mine, width : width + quarter] = tail.astype(bf16)
    buf[mine, width + quarter :] = (mm(head, lanes(0)) + mm(rest[0], lanes(4))).astype(bf16)

    pl.semaphore_wait(barrier, len(peers))

    def copy(slot, sem, peer):
        piece = buf.at[pl.ds(pl.multiple_of(slot * 16, 16), 16)]
        return pltpu.make_async_remote_copy(
            src_ref=piece, dst_ref=piece, send_sem=send_sem.at[sem], recv_sem=recv_sem.at[slot],
            device_id=peer, device_id_type=pl.DeviceIdType.MESH,
        )

    def onward(k, flip_a, flip_b):
        slot = slot_of(z if k == 0 else line[k - 1], flip_a, flip_b)
        out = []
        if not flip_a and not flip_b:
            if k == 0:
                for n, zz in enumerate(line):
                    out.append(copy(slot, n, (zz * 2 + y, inner)))
            out.append(copy(slot, depth + k, peer_a))
            out.append(copy(slot, 2 * depth + k, peer_b))
            out.append(copy(slot, 3 * depth + k, peer_diag))
        out.append(copy(slot, (4 + 2 * flip_b + flip_a) * depth + k, peer_core))
        return slot, out

    def arrive(slot):
        copy(slot, 0, peer_core).wait_recv()

    order = sorted((k + (flip_a + flip_b), flip_a + flip_b, k, flip_a, flip_b)
                   for k in range(depth) for flip_a in (0, 1) for flip_b in (0, 1))
    started = []
    for _, hops, k, flip_a, flip_b in order:
        slot, copies = onward(k, flip_a, flip_b)
        if k or hops:
            arrive(slot)
        for one in copies:
            one.start()
        started += copies

    def from_core(zz, carry):
        for fb in (0, 1):
            for fa in (0, 1):
                s = slot_of(zz, fa, fb)
                arrive(s + 1 - 2 * core)
        return carry

    lax.fori_loop(0, depth, from_core, 0)

    count = 2 * rows * buf.shape[0] // 16
    heads = buf.shape[0]
    tails = count - heads
    rows_all[0:heads, :] = buf[:, 0:width]
    left = buf[:, width : width + quarter]
    meta = buf[:, width + quarter :]
    picks = [
        select((tails, heads), lambda r, c, k=k: c == r // 4 * 16 + k * 4 + r % 4) for k in range(4)
    ]
    for k in range(4):
        rows_all[heads:, k * quarter : (k + 1) * quarter] = mm(picks[k], left).astype(bf16)
    meta_tail = mm(picks[0], meta).astype(bf16)

    def reader(first, axis, shape):
        pos = lax.broadcasted_iota(jnp.int32, shape, axis)
        return jnp.where(pos == first, 32.0, jnp.where(pos == first + 1, 1.0, 0.0)).astype(bf16)

    for ref, first in ((scol, 0), (ucol, 2)):
        ref[0:heads, :] = mm(meta, reader(first, 0, (128, 128)))
        ref[heads:, :] = mm(meta_tail, reader(first + 4, 0, (128, 128)))
    for ref, first in ((srow, 0), (urow, 2)):
        ref[:, 0:heads] = mmt(reader(first, 1, (8, 128)), meta)
        ref[:, heads:] = mmt(reader(first + 4, 1, (8, 128)), meta_tail)
    s_row, u_row = srow[0:1, :], urow[0:1, :]
    lse_self[...] = jnp.zeros_like(lse_self)
    lse_pair[...] = jnp.zeros_like(lse_pair)
    chunk = count

    def forward(step, carry):
        at = pl.ds(pl.multiple_of(step * chunk, chunk), chunk)
        scores = mmt(rows_all[at, :], rows_all[...]) * INV_TAU
        apart = u_row - ucol[at, 0:1]
        allowed = (apart == 0.25) | ((s_row != scol[at, 0:1]) & (apart != -0.25))
        scores = jnp.where(allowed, scores, NEG)
        peak = jnp.max(scores, axis=1, keepdims=True)
        total = jnp.sum(jnp.exp(scores - peak), axis=1, keepdims=True)
        lse = jnp.where(peak > 0.5 * NEG, peak + jnp.log(total), NEG)
        lse_self[0:1, :] += jnp.sum(jnp.where(apart == 0.0, lse, 0.0), axis=0, keepdims=True)
        lse_pair[0:1, :] += jnp.sum(
            jnp.where(jnp.abs(apart) == 0.25, lse, 0.0), axis=0, keepdims=True
        )
        return carry

    lax.fori_loop(0, count // chunk, forward, 0)
    first, second = lse_self[0:1, :], lse_pair[0:1, :]
    norm_row = jnp.maximum(first, second) + jnp.log(1.0 + jnp.exp(-jnp.abs(first - second)))

    scores = mmt(own, rows_all[...]) * INV_TAU
    apart = u_row - own_key[:, 0:1]
    hit = jnp.abs(apart) == 0.25
    norm_own = jnp.sum(jnp.where(apart == 0.0, norm_row, 0.0), axis=1, keepdims=True)
    loss = norm_own - jnp.sum(jnp.where(hit, scores, 0.0), axis=1, keepdims=True)
    loss_ref[...] = jnp.broadcast_to(loss, loss_ref.shape)
    from_own = jnp.exp(scores - norm_own)
    apart_source = (s_row != own_source[:, 0:1]) & (own_key[:, 0:1] >= 0.0)
    weights = jnp.where(
        hit, from_own - 1.0, jnp.where(apart_source, from_own + jnp.exp(scores - norm_row), 0.0)
    )
    grads = mm(weights.astype(bf16), rows_all[...]) * INV_TAU
    unit = unit_own[...]
    grads = (grads - unit * jnp.sum(unit * grads, axis=1, keepdims=True)) / len_own[:, 0:1]
    gq_ref[...] = grads[0:rows, :]
    gd_ref[...] = grads[16 : 16 + rows, :]

    for one in started:
        one.wait_send()


def whole_batch(depth, query_emb, doc_emb, positive, query_source, doc_source):
    rows, width = query_emb.shape
    devices = lax.axis_size("blk") * lax.axis_size("inner")
    count = 2 * rows * devices
    vmem = pl.BlockSpec(memory_space=pltpu.VMEM)
    f32 = jnp.float32
    loss, grad_query, grad_doc = pl.pallas_call(
        functools.partial(gather_kernel, depth),
        out_shape=(
            jax.ShapeDtypeStruct((32, 128), f32),
            jax.ShapeDtypeStruct((rows, width), f32),
            jax.ShapeDtypeStruct((rows, width), f32),
        ),
        in_specs=[pl.BlockSpec(memory_space=pltpu.HBM)] * 5,
        out_specs=(vmem, vmem, vmem),
        scratch_shapes=[
            pltpu.VMEM((rows, width), jnp.bfloat16),
            pltpu.VMEM((rows, width), jnp.bfloat16),
            pltpu.SMEM((rows,), jnp.int32),
            pltpu.SMEM((rows,), jnp.int32),
            pltpu.SMEM((rows,), jnp.int32),
            pltpu.SemaphoreType.DMA((5,)),
            pltpu.VMEM((devices * 16, width + width // 4 + 128), jnp.bfloat16),
            pltpu.VMEM((count, width), jnp.bfloat16),
            pltpu.VMEM((32, width), f32),
            pltpu.VMEM((32, 128), f32),
            pltpu.VMEM((count, 128), f32),
            pltpu.VMEM((count, 128), f32),
            pltpu.VMEM((8, count), f32),
            pltpu.VMEM((8, count), f32),
            pltpu.VMEM((8, count), f32),
            pltpu.VMEM((8, count), f32),
            pltpu.SemaphoreType.DMA((8 * depth,)),
            pltpu.SemaphoreType.DMA((devices,)),
        ],
        compiler_params=pltpu.CompilerParams(
            collective_id=0, has_side_effects=True, vmem_limit_bytes=40 * 1024 * 1024
        ),
    )(query_emb, doc_emb, positive, query_source, doc_source)
    return (loss[:rows, 0], grad_query, grad_doc)


def solution(mesh):
    small = mesh.shape["inner"] == 4 and mesh.shape["blk"] == 8
    body = functools.partial(whole_batch, mesh.shape["blk"] // 2) if small else shards
    placed = (
        P(("blk", "inner"), None),
        P(("blk", "inner"), None),
        P(("blk", "inner")),
        P(("blk", "inner")),
        P(("blk", "inner")),
    )
    return jax.shard_map(
        body,
        mesh=mesh,
        in_specs=placed,
        out_specs=(P(("blk", "inner")), P(("blk", "inner"), None), P(("blk", "inner"), None)),
        check_vma=False,
    )
```

```python
import functools

import jax
import jax.numpy as jnp
from jax import lax
from jax.experimental import pallas as pl
from jax.experimental.pallas import tpu as pltpu
from jax.sharding import PartitionSpec as P

EPS = 1e-06
INV_TAU = 100.0
NEG = -1e30


def joined_2(value, axis, join):
    pieces = jax.tree.map(lambda part: lax.all_gather(part, axis), value)
    head = jax.tree.map(lambda part: part[0], pieces)
    tail = jax.tree.map(lambda part: part[1:], pieces)
    so_far, _ = lax.scan(lambda so_far, piece: (join(so_far, piece), None), head, tail)
    return so_far


def unit_rows(values):
    widened = values.astype(jnp.float32)
    lengths = jnp.sqrt(jnp.sum(widened * widened, axis=1, keepdims=True) + EPS)
    return (widened / lengths, lengths)


def scaled_gram(left_rows, right_rows):
    return (
        lax.dot_general(
            left_rows, right_rows, (((1,), (1,)), ((), ())), preferred_element_type=jnp.float32
        )
        * INV_TAU
    )


def pair_masks(row_info, col_info):
    row_qsource, row_dsource, row_target, row_global = row_info
    col_qsource, col_dsource, col_target, col_global = col_info
    mask_qd = (col_global[None, :] == row_target[:, None]) | (
        col_dsource[None, :] != row_qsource[:, None]
    )
    mask_dq = (col_target[None, :] != row_global[:, None]) & (
        col_qsource[None, :] != row_dsource[:, None]
    )
    mask_qq = col_qsource[None, :] != row_qsource[:, None]
    mask_dd = col_dsource[None, :] != row_dsource[:, None]
    twin_dq = (row_target[:, None] != col_global[None, :]) & (
        row_qsource[:, None] != col_dsource[None, :]
    )
    twin_qd = (row_global[:, None] == col_target[None, :]) | (
        row_dsource[:, None] != col_qsource[None, :]
    )
    return (mask_qd, mask_dq, mask_qq, mask_dd, twin_dq, twin_qd)


def masked_terms(scores_list, masks_list):
    peak = jnp.max(jnp.where(masks_list[0], scores_list[0], NEG), axis=1)
    for scores, masked in zip(scores_list[1:], masks_list[1:]):
        peak = jnp.maximum(peak, jnp.max(jnp.where(masked, scores, NEG), axis=1))
    totals = jnp.zeros(peak.shape, jnp.float32)
    for scores, masked in zip(scores_list, masks_list):
        totals = totals + jnp.sum(jnp.exp(jnp.where(masked, scores - peak[:, None], NEG)), axis=1)
    return (peak, totals)


def joined(former, latter):
    peak = jnp.maximum(former[0], latter[0])
    return (peak, former[1] * jnp.exp(former[0] - peak) + latter[1] * jnp.exp(latter[0] - peak))


def merge_stats(former, latter):
    query_pair = joined((former[0], former[1]), (latter[0], latter[1]))
    doc_pair = joined((former[2], former[3]), (latter[2], latter[3]))
    return (query_pair[0], query_pair[1], doc_pair[0], doc_pair[1], former[4] + latter[4])


def column_global(offset, amount, rows_dev, inner_count, inner_pos):
    flat = offset + jnp.arange(amount, dtype=jnp.int32)
    return flat // rows_dev * (inner_count * rows_dev) + inner_pos * rows_dev + flat % rows_dev


def weight(masked, scores, norms):
    return jnp.exp(jnp.where(masked, scores - norms, NEG))


def weighted(weights, right_rows):
    return jnp.dot(weights.astype(jnp.bfloat16), right_rows, preferred_element_type=jnp.float32)


def shards(query_emb, doc_emb, positive, query_source, doc_source):
    rows_dev = query_emb.shape[0]
    inner_count = lax.axis_size("inner")
    inner_pos = lax.axis_index("inner")
    blk_pos = lax.axis_index("blk")
    group_base = blk_pos * inner_count * rows_dev
    unit_query, query_len = unit_rows(query_emb)
    unit_doc, doc_len = unit_rows(doc_emb)
    query_half = unit_query.astype(jnp.bfloat16)
    doc_half = unit_doc.astype(jnp.bfloat16)
    row_query, row_doc, row_qsource, row_dsource, row_target = (
        lax.all_gather(query_half, "inner", axis=0, tiled=True),
        lax.all_gather(doc_half, "inner", axis=0, tiled=True),
        lax.all_gather(query_source, "inner", axis=0, tiled=True),
        lax.all_gather(doc_source, "inner", axis=0, tiled=True),
        lax.all_gather(positive, "inner", axis=0, tiled=True),
    )
    row_global = group_base + jnp.arange(row_query.shape[0], dtype=jnp.int32)
    own_start = inner_pos * rows_dev

    def col_index(offset, amount):
        return column_global(offset, amount, rows_dev, inner_count, inner_pos)

    row_count = row_query.shape[0]
    row_info = (row_qsource, row_dsource, row_target, row_global)

    def tile(pieces, offset):
        col_query, col_doc, col_qsource, col_dsource, col_target = pieces
        col_global = col_index(offset, col_query.shape[0])
        scores = (
            scaled_gram(row_query, col_doc),
            scaled_gram(row_doc, col_query),
            scaled_gram(row_query, col_query),
            scaled_gram(row_doc, col_doc),
        )
        masks = pair_masks(row_info, (col_qsource, col_dsource, col_target, col_global))
        return (col_global, scores, masks)

    empty_peak = jnp.full((row_count,), NEG, jnp.float32)
    empty_sum = jnp.zeros((row_count,), jnp.float32)
    start_stats = (empty_peak, empty_sum, empty_peak, empty_sum, empty_sum)
    columns = (
        lax.all_gather(query_half, "blk", axis=0, tiled=True),
        lax.all_gather(doc_half, "blk", axis=0, tiled=True),
        lax.all_gather(query_source, "blk", axis=0, tiled=True),
        lax.all_gather(doc_source, "blk", axis=0, tiled=True),
        lax.all_gather(positive, "blk", axis=0, tiled=True),
    )
    col_global, scores, masks = tile(columns, 0)
    query_side = masked_terms([scores[0], scores[2]], [masks[0], masks[2]])
    doc_side = masked_terms([scores[1], scores[3]], [masks[1], masks[3]])
    hit = jnp.sum(jnp.where(col_global[None, :] == row_target[:, None], scores[0], 0.0), axis=1)
    stats = merge_stats(start_stats, (query_side[0], query_side[1], doc_side[0], doc_side[1], hit))
    stats = joined_2(stats, "inner", merge_stats)
    query_lse = stats[0] + jnp.log(stats[1])
    doc_lse = stats[2] + jnp.log(stats[3])
    own_doc_lse = lax.dynamic_slice_in_dim(doc_lse, own_start, rows_dev, 0)
    doc_lse_all, target_all = (
        lax.all_gather(own_doc_lse, ("blk", "inner"), axis=0, tiled=True),
        lax.all_gather(positive, ("blk", "inner"), axis=0, tiled=True),
    )
    own_query_lse = lax.dynamic_slice_in_dim(query_lse, own_start, rows_dev, 0)
    own_hit = lax.dynamic_slice_in_dim(stats[4], own_start, rows_dev, 0)
    own_norm = jnp.logaddexp(own_query_lse, jnp.take(doc_lse_all, positive))
    row_loss = own_norm - own_hit
    norm_all = lax.all_gather(own_norm, ("blk", "inner"), axis=0, tiled=True)
    pairs = norm_all.shape[0]
    inverse = jnp.zeros((pairs,), jnp.int32).at[target_all].set(jnp.arange(pairs, dtype=jnp.int32))
    doc_norm_all = jnp.take(norm_all, inverse)
    row_norm = jnp.take(norm_all, row_global)[:, None]
    row_doc_norm = jnp.take(doc_norm_all, row_global)[:, None]
    col_global, scores, masks = tile(columns, 0)
    col_query = columns[0]
    col_doc = columns[1]
    col_target = columns[4]
    col_norm = jnp.take(norm_all, col_global)[None, :]
    col_doc_norm = jnp.take(doc_norm_all, col_global)[None, :]
    qd_weight = (
        weight(masks[0], scores[0], row_norm)
        + weight(masks[4], scores[0], col_doc_norm)
        - (col_global[None, :] == row_target[:, None]).astype(jnp.float32)
    )
    qq_weight = weight(masks[2], scores[2], row_norm) + weight(masks[2], scores[2], col_norm)
    dq_weight = (
        weight(masks[1], scores[1], row_doc_norm)
        + weight(masks[5], scores[1], col_norm)
        - (col_target[None, :] == row_global[:, None]).astype(jnp.float32)
    )
    dd_weight = weight(masks[3], scores[3], row_doc_norm) + weight(
        masks[3], scores[3], col_doc_norm
    )
    query_grad = (weighted(qd_weight, col_doc) + weighted(qq_weight, col_query)) * INV_TAU
    doc_grad = (weighted(dq_weight, col_query) + weighted(dd_weight, col_doc)) * INV_TAU
    query_part, doc_part = (
        lax.psum_scatter(query_grad, "inner", scatter_dimension=0, tiled=True),
        lax.psum_scatter(doc_grad, "inner", scatter_dimension=0, tiled=True),
    )
    grad_query = (
        query_part - unit_query * jnp.sum(unit_query * query_part, axis=1, keepdims=True)
    ) / query_len
    grad_doc = (doc_part - unit_doc * jnp.sum(unit_doc * doc_part, axis=1, keepdims=True)) / doc_len
    return (row_loss, grad_query, grad_doc)


def gather_kernel(
    depth, q_hbm, d_hbm, pos_hbm, qs_hbm, ds_hbm, loss_ref, gq_ref, gd_ref,
    q_ref, d_ref, pos_ref, qs_ref, ds_ref, in_sem, buf, rows_all, unit_own, len_own, scol, ucol, srow, urow, lse_self, lse_pair, send_sem, recv_sem,
):
    f32, bf16 = jnp.float32, jnp.bfloat16
    rows = q_ref.shape[0]
    width = q_ref.shape[1]
    quarter = width // 4
    blk, inner = lax.axis_index("blk"), lax.axis_index("inner")
    z, y = blk // 2, blk % 2
    x, core = inner // 2, inner % 2
    me = blk * 4 + inner

    def place(zz, flip_a, flip_b):
        flip_y = flip_a * (1 - core) + flip_b * core
        flip_x = flip_a * core + flip_b * (1 - core)
        yy = y + flip_y * (1 - 2 * y)
        xx = x + flip_x * (1 - 2 * x)
        return zz * 2 + yy, xx * 2 + core

    def slot_of(zz, flip_a, flip_b):
        b, i = place(zz, flip_a, flip_b)
        return b * 4 + i

    peer_a = place(z, 1, 0)
    peer_b = place(z, 0, 1)
    peer_diag = place(z, 1, 1)
    peer_core = (blk, x * 2 + 1 - core)
    upper = z // (depth // 2)
    low = z * (1 - upper) + (depth - 1 - z) * upper

    def near(k):
        kth = k + jnp.minimum(jnp.maximum(k - low + 1, 0), 1)
        return kth * (1 - upper) + (depth - 1 - kth) * upper

    line = [near(k) for k in range(depth - 1)]

    barrier = pltpu.get_barrier_semaphore()
    peers = [(zz * 2 + y, inner) for zz in line] + [peer_a, peer_b, peer_diag, peer_core]
    for peer in peers:
        pl.semaphore_signal(barrier, inc=1, device_id=peer, device_id_type=pl.DeviceIdType.MESH)

    held = ((q_hbm, q_ref), (d_hbm, d_ref), (pos_hbm, pos_ref), (qs_hbm, qs_ref), (ds_hbm, ds_ref))
    loads = [pltpu.make_async_copy(a, b, in_sem.at[n]) for n, (a, b) in enumerate(held)]
    for load in loads:
        load.start()
    for load in loads:
        load.wait()
    unit_own[...] = jnp.zeros_like(unit_own)
    len_own[...] = jnp.ones_like(len_own)
    for ref, first in ((q_ref, 0), (d_ref, 16)):
        wide = ref[...].astype(f32)
        lengths = jnp.sqrt(jnp.sum(wide * wide, axis=1, keepdims=True) + EPS)
        unit_own[pl.ds(first, rows), :] = wide / lengths
        len_own[pl.ds(first, rows), :] = jnp.broadcast_to(lengths, (rows, 128))
    own = unit_own[...].astype(bf16)

    row = lax.broadcasted_iota(jnp.int32, (32, 128), 0)
    lane = lax.broadcasted_iota(jnp.int32, (32, 128), 1)
    source = jnp.zeros((32, 128), jnp.int32)
    key = jnp.zeros((32, 128), jnp.int32)
    for r in range(rows):
        source = jnp.where(row == r, qs_ref[r], source)
        source = jnp.where(row == 16 + r, ds_ref[r], source)
        key = jnp.where(row == r, pos_ref[r], key)
    key = jnp.where(row >= 16, me * rows + row - 16, key)
    kind = jnp.where(row >= 16, 0.25, 0.0).astype(f32)
    valid = (row % 16) < rows
    own_source = source.astype(f32)
    own_key = jnp.where(valid, key.astype(f32) + kind, -100.0)
    parts = (
        (source >> 5).astype(f32),
        (source & 31).astype(f32),
        (key >> 5).astype(f32),
        (key & 31).astype(f32) + kind,
    )

    def lanes(first):
        out = jnp.zeros((32, 128), f32)
        for k, part in enumerate(parts):
            out = jnp.where(lane == first + k, part, out)
        return out.astype(bf16)

    def select(shape, chosen):
        r = lax.broadcasted_iota(jnp.int32, shape, 0)
        c = lax.broadcasted_iota(jnp.int32, shape, 1)
        return chosen(r, c).astype(f32).astype(bf16)

    def mm(a, b):
        return jnp.dot(a, b, preferred_element_type=f32)

    def mmt(a, b):
        return lax.dot_general(a, b, (((1,), (1,)), ((), ())), preferred_element_type=f32)

    head = select((16, 32), lambda r, c: c == jnp.where(r < rows, r, r + 16 - rows))
    rest = [
        select((16, 32), lambda r, c, k=k: (r // 4 == k) & (c == 32 - rows + r % 4)) for k in range(4)
    ]
    mine = pl.ds(pl.multiple_of(me * 16, 16), 16)
    buf[mine, 0:width] = mm(head, own).astype(bf16)
    tail = mm(rest[0], own[:, 0:quarter])
    for k in range(1, 4):
        tail = tail + mm(rest[k], own[:, k * quarter : (k + 1) * quarter])
    buf[mine, width : width + quarter] = tail.astype(bf16)
    buf[mine, width + quarter :] = (mm(head, lanes(0)) + mm(rest[0], lanes(4))).astype(bf16)

    pl.semaphore_wait(barrier, len(peers))

    def copy(slot, sem, peer):
        piece = buf.at[pl.ds(pl.multiple_of(slot * 16, 16), 16)]
        return pltpu.make_async_remote_copy(
            src_ref=piece, dst_ref=piece, send_sem=send_sem.at[sem], recv_sem=recv_sem.at[slot],
            device_id=peer, device_id_type=pl.DeviceIdType.MESH,
        )

    def onward(k, flip_a, flip_b):
        slot = slot_of(z if k == 0 else line[k - 1], flip_a, flip_b)
        out = []
        if not flip_a and not flip_b:
            if k == 0:
                for n, zz in enumerate(line):
                    out.append(copy(slot, n, (zz * 2 + y, inner)))
            out.append(copy(slot, depth + k, peer_a))
            out.append(copy(slot, 2 * depth + k, peer_b))
            out.append(copy(slot, 3 * depth + k, peer_diag))
        out.append(copy(slot, (4 + 2 * flip_b + flip_a) * depth + k, peer_core))
        return slot, out

    def arrive(slot):
        copy(slot, 0, peer_core).wait_recv()

    order = sorted((k + (flip_a + flip_b), flip_a + flip_b, k, flip_a, flip_b)
                   for k in range(depth) for flip_a in (0, 1) for flip_b in (0, 1))
    started = []
    for _, hops, k, flip_a, flip_b in order:
        slot, copies = onward(k, flip_a, flip_b)
        if k or hops:
            arrive(slot)
        for one in copies:
            one.start()
        started += copies

    def from_core(zz, carry):
        for fb in (0, 1):
            for fa in (0, 1):
                s = slot_of(zz, fa, fb)
                arrive(s + 1 - 2 * core)
        return carry

    lax.fori_loop(0, depth, from_core, 0)

    count = 2 * rows * buf.shape[0] // 16
    heads = buf.shape[0]
    tails = count - heads
    rows_all[0:heads, :] = buf[:, 0:width]
    left = buf[:, width : width + quarter]
    meta = buf[:, width + quarter :]
    picks = [
        select((tails, heads), lambda r, c, k=k: c == r // 4 * 16 + k * 4 + r % 4) for k in range(4)
    ]
    for k in range(4):
        rows_all[heads:, k * quarter : (k + 1) * quarter] = mm(picks[k], left).astype(bf16)
    meta_tail = mm(picks[0], meta).astype(bf16)

    def reader(first, axis, shape):
        pos = lax.broadcasted_iota(jnp.int32, shape, axis)
        return jnp.where(pos == first, 32.0, jnp.where(pos == first + 1, 1.0, 0.0)).astype(bf16)

    for ref, first in ((scol, 0), (ucol, 2)):
        ref[0:heads, :] = mm(meta, reader(first, 0, (128, 128)))
        ref[heads:, :] = mm(meta_tail, reader(first + 4, 0, (128, 128)))
    for ref, first in ((srow, 0), (urow, 2)):
        ref[:, 0:heads] = mmt(reader(first, 1, (8, 128)), meta)
        ref[:, heads:] = mmt(reader(first + 4, 1, (8, 128)), meta_tail)
    s_row, u_row = srow[0:1, :], urow[0:1, :]
    lse_self[...] = jnp.zeros_like(lse_self)
    lse_pair[...] = jnp.zeros_like(lse_pair)
    chunk = count

    def forward(step, carry):
        at = pl.ds(pl.multiple_of(step * chunk, chunk), chunk)
        scores = mmt(rows_all[at, :], rows_all[...]) * INV_TAU
        apart = u_row - ucol[at, 0:1]
        allowed = (apart == 0.25) | ((s_row != scol[at, 0:1]) & (apart != -0.25))
        scores = jnp.where(allowed, scores, NEG)
        peak = jnp.max(scores, axis=1, keepdims=True)
        total = jnp.sum(jnp.exp(scores - peak), axis=1, keepdims=True)
        lse = jnp.where(peak > 0.5 * NEG, peak + jnp.log(total), NEG)
        lse_self[0:1, :] += jnp.sum(jnp.where(apart == 0.0, lse, 0.0), axis=0, keepdims=True)
        lse_pair[0:1, :] += jnp.sum(
            jnp.where(jnp.abs(apart) == 0.25, lse, 0.0), axis=0, keepdims=True
        )
        return carry

    lax.fori_loop(0, count // chunk, forward, 0)
    first, second = lse_self[0:1, :], lse_pair[0:1, :]
    norm_row = jnp.maximum(first, second) + jnp.log(1.0 + jnp.exp(-jnp.abs(first - second)))

    scores = mmt(own, rows_all[...]) * INV_TAU
    apart = u_row - own_key[:, 0:1]
    hit = jnp.abs(apart) == 0.25
    norm_own = jnp.sum(jnp.where(apart == 0.0, norm_row, 0.0), axis=1, keepdims=True)
    loss = norm_own - jnp.sum(jnp.where(hit, scores, 0.0), axis=1, keepdims=True)
    loss_ref[...] = jnp.broadcast_to(loss, loss_ref.shape)
    from_own = jnp.exp(scores - norm_own)
    apart_source = (s_row != own_source[:, 0:1]) & (own_key[:, 0:1] >= 0.0)
    weights = jnp.where(
        hit, from_own - 1.0, jnp.where(apart_source, from_own + jnp.exp(scores - norm_row), 0.0)
    )
    grads = mm(weights.astype(bf16), rows_all[...]) * INV_TAU
    unit = unit_own[...]
    grads = (grads - unit * jnp.sum(unit * grads, axis=1, keepdims=True)) / len_own[:, 0:1]
    gq_ref[...] = grads[0:rows, :]
    gd_ref[...] = grads[16 : 16 + rows, :]

    for one in started:
        one.wait_send()


def whole_batch(depth, query_emb, doc_emb, positive, query_source, doc_source):
    rows, width = query_emb.shape
    devices = lax.axis_size("blk") * lax.axis_size("inner")
    count = 2 * rows * devices
    vmem = pl.BlockSpec(memory_space=pltpu.VMEM)
    f32 = jnp.float32
    loss, grad_query, grad_doc = pl.pallas_call(
        functools.partial(gather_kernel, depth),
        out_shape=(
            jax.ShapeDtypeStruct((32, 128), f32),
            jax.ShapeDtypeStruct((rows, width), f32),
            jax.ShapeDtypeStruct((rows, width), f32),
        ),
        in_specs=[pl.BlockSpec(memory_space=pltpu.HBM)] * 5,
        out_specs=(vmem, vmem, vmem),
        scratch_shapes=[
            pltpu.VMEM((rows, width), jnp.bfloat16),
            pltpu.VMEM((rows, width), jnp.bfloat16),
            pltpu.SMEM((rows,), jnp.int32),
            pltpu.SMEM((rows,), jnp.int32),
            pltpu.SMEM((rows,), jnp.int32),
            pltpu.SemaphoreType.DMA((5,)),
            pltpu.VMEM((devices * 16, width + width // 4 + 128), jnp.bfloat16),
            pltpu.VMEM((count, width), jnp.bfloat16),
            pltpu.VMEM((32, width), f32),
            pltpu.VMEM((32, 128), f32),
            pltpu.VMEM((count, 128), f32),
            pltpu.VMEM((count, 128), f32),
            pltpu.VMEM((8, count), f32),
            pltpu.VMEM((8, count), f32),
            pltpu.VMEM((8, count), f32),
            pltpu.VMEM((8, count), f32),
            pltpu.SemaphoreType.DMA((8 * depth,)),
            pltpu.SemaphoreType.DMA((devices,)),
        ],
        compiler_params=pltpu.CompilerParams(
            collective_id=0, has_side_effects=True, vmem_limit_bytes=56 * 1024 * 1024
        ),
    )(query_emb, doc_emb, positive, query_source, doc_source)
    return (loss[:rows, 0], grad_query, grad_doc)


def solution(mesh):
    small = mesh.shape["inner"] == 4 and mesh.shape["blk"] == 8
    body = functools.partial(whole_batch, mesh.shape["blk"] // 2) if small else shards
    placed = (
        P(("blk", "inner"), None),
        P(("blk", "inner"), None),
        P(("blk", "inner")),
        P(("blk", "inner")),
        P(("blk", "inner")),
    )
    return jax.shard_map(
        body,
        mesh=mesh,
        in_specs=placed,
        out_specs=(P(("blk", "inner")), P(("blk", "inner"), None), P(("blk", "inner"), None)),
        check_vma=False,
    )
```

```python
import functools

import jax
import jax.numpy as jnp
from jax import lax
from jax.experimental import pallas as pl
from jax.experimental.pallas import tpu as pltpu
from jax.sharding import PartitionSpec as P

EPS = 1e-06
INV_TAU = 100.0
NEG = -1e30


def joined_2(value, axis, join):
    pieces = jax.tree.map(lambda part: lax.all_gather(part, axis), value)
    head = jax.tree.map(lambda part: part[0], pieces)
    tail = jax.tree.map(lambda part: part[1:], pieces)
    so_far, _ = lax.scan(lambda so_far, piece: (join(so_far, piece), None), head, tail)
    return so_far


def unit_rows(values):
    widened = values.astype(jnp.float32)
    lengths = jnp.sqrt(jnp.sum(widened * widened, axis=1, keepdims=True) + EPS)
    return (widened / lengths, lengths)


def scaled_gram(left_rows, right_rows):
    return (
        lax.dot_general(
            left_rows, right_rows, (((1,), (1,)), ((), ())), preferred_element_type=jnp.float32
        )
        * INV_TAU
    )


def pair_masks(row_info, col_info):
    row_qsource, row_dsource, row_target, row_global = row_info
    col_qsource, col_dsource, col_target, col_global = col_info
    mask_qd = (col_global[None, :] == row_target[:, None]) | (
        col_dsource[None, :] != row_qsource[:, None]
    )
    mask_dq = (col_target[None, :] != row_global[:, None]) & (
        col_qsource[None, :] != row_dsource[:, None]
    )
    mask_qq = col_qsource[None, :] != row_qsource[:, None]
    mask_dd = col_dsource[None, :] != row_dsource[:, None]
    twin_dq = (row_target[:, None] != col_global[None, :]) & (
        row_qsource[:, None] != col_dsource[None, :]
    )
    twin_qd = (row_global[:, None] == col_target[None, :]) | (
        row_dsource[:, None] != col_qsource[None, :]
    )
    return (mask_qd, mask_dq, mask_qq, mask_dd, twin_dq, twin_qd)


def masked_terms(scores_list, masks_list):
    peak = jnp.max(jnp.where(masks_list[0], scores_list[0], NEG), axis=1)
    for scores, masked in zip(scores_list[1:], masks_list[1:]):
        peak = jnp.maximum(peak, jnp.max(jnp.where(masked, scores, NEG), axis=1))
    totals = jnp.zeros(peak.shape, jnp.float32)
    for scores, masked in zip(scores_list, masks_list):
        totals = totals + jnp.sum(jnp.exp(jnp.where(masked, scores - peak[:, None], NEG)), axis=1)
    return (peak, totals)


def joined(former, latter):
    peak = jnp.maximum(former[0], latter[0])
    return (peak, former[1] * jnp.exp(former[0] - peak) + latter[1] * jnp.exp(latter[0] - peak))


def merge_stats(former, latter):
    query_pair = joined((former[0], former[1]), (latter[0], latter[1]))
    doc_pair = joined((former[2], former[3]), (latter[2], latter[3]))
    return (query_pair[0], query_pair[1], doc_pair[0], doc_pair[1], former[4] + latter[4])


def column_global(offset, amount, rows_dev, inner_count, inner_pos):
    flat = offset + jnp.arange(amount, dtype=jnp.int32)
    return flat // rows_dev * (inner_count * rows_dev) + inner_pos * rows_dev + flat % rows_dev


def weight(masked, scores, norms):
    return jnp.exp(jnp.where(masked, scores - norms, NEG))


def weighted(weights, right_rows):
    return jnp.dot(weights.astype(jnp.bfloat16), right_rows, preferred_element_type=jnp.float32)


def shards(query_emb, doc_emb, positive, query_source, doc_source):
    rows_dev = query_emb.shape[0]
    inner_count = lax.axis_size("inner")
    inner_pos = lax.axis_index("inner")
    blk_pos = lax.axis_index("blk")
    group_base = blk_pos * inner_count * rows_dev
    unit_query, query_len = unit_rows(query_emb)
    unit_doc, doc_len = unit_rows(doc_emb)
    query_half = unit_query.astype(jnp.bfloat16)
    doc_half = unit_doc.astype(jnp.bfloat16)
    row_query, row_doc, row_qsource, row_dsource, row_target = (
        lax.all_gather(query_half, "inner", axis=0, tiled=True),
        lax.all_gather(doc_half, "inner", axis=0, tiled=True),
        lax.all_gather(query_source, "inner", axis=0, tiled=True),
        lax.all_gather(doc_source, "inner", axis=0, tiled=True),
        lax.all_gather(positive, "inner", axis=0, tiled=True),
    )
    row_global = group_base + jnp.arange(row_query.shape[0], dtype=jnp.int32)
    own_start = inner_pos * rows_dev

    def col_index(offset, amount):
        return column_global(offset, amount, rows_dev, inner_count, inner_pos)

    row_count = row_query.shape[0]
    row_info = (row_qsource, row_dsource, row_target, row_global)

    def tile(pieces, offset):
        col_query, col_doc, col_qsource, col_dsource, col_target = pieces
        col_global = col_index(offset, col_query.shape[0])
        scores = (
            scaled_gram(row_query, col_doc),
            scaled_gram(row_doc, col_query),
            scaled_gram(row_query, col_query),
            scaled_gram(row_doc, col_doc),
        )
        masks = pair_masks(row_info, (col_qsource, col_dsource, col_target, col_global))
        return (col_global, scores, masks)

    empty_peak = jnp.full((row_count,), NEG, jnp.float32)
    empty_sum = jnp.zeros((row_count,), jnp.float32)
    start_stats = (empty_peak, empty_sum, empty_peak, empty_sum, empty_sum)
    columns = (
        lax.all_gather(query_half, "blk", axis=0, tiled=True),
        lax.all_gather(doc_half, "blk", axis=0, tiled=True),
        lax.all_gather(query_source, "blk", axis=0, tiled=True),
        lax.all_gather(doc_source, "blk", axis=0, tiled=True),
        lax.all_gather(positive, "blk", axis=0, tiled=True),
    )
    col_global, scores, masks = tile(columns, 0)
    query_side = masked_terms([scores[0], scores[2]], [masks[0], masks[2]])
    doc_side = masked_terms([scores[1], scores[3]], [masks[1], masks[3]])
    hit = jnp.sum(jnp.where(col_global[None, :] == row_target[:, None], scores[0], 0.0), axis=1)
    stats = merge_stats(start_stats, (query_side[0], query_side[1], doc_side[0], doc_side[1], hit))
    stats = joined_2(stats, "inner", merge_stats)
    query_lse = stats[0] + jnp.log(stats[1])
    doc_lse = stats[2] + jnp.log(stats[3])
    own_doc_lse = lax.dynamic_slice_in_dim(doc_lse, own_start, rows_dev, 0)
    doc_lse_all, target_all = (
        lax.all_gather(own_doc_lse, ("blk", "inner"), axis=0, tiled=True),
        lax.all_gather(positive, ("blk", "inner"), axis=0, tiled=True),
    )
    own_query_lse = lax.dynamic_slice_in_dim(query_lse, own_start, rows_dev, 0)
    own_hit = lax.dynamic_slice_in_dim(stats[4], own_start, rows_dev, 0)
    own_norm = jnp.logaddexp(own_query_lse, jnp.take(doc_lse_all, positive))
    row_loss = own_norm - own_hit
    norm_all = lax.all_gather(own_norm, ("blk", "inner"), axis=0, tiled=True)
    pairs = norm_all.shape[0]
    inverse = jnp.zeros((pairs,), jnp.int32).at[target_all].set(jnp.arange(pairs, dtype=jnp.int32))
    doc_norm_all = jnp.take(norm_all, inverse)
    row_norm = jnp.take(norm_all, row_global)[:, None]
    row_doc_norm = jnp.take(doc_norm_all, row_global)[:, None]
    col_global, scores, masks = tile(columns, 0)
    col_query = columns[0]
    col_doc = columns[1]
    col_target = columns[4]
    col_norm = jnp.take(norm_all, col_global)[None, :]
    col_doc_norm = jnp.take(doc_norm_all, col_global)[None, :]
    qd_weight = (
        weight(masks[0], scores[0], row_norm)
        + weight(masks[4], scores[0], col_doc_norm)
        - (col_global[None, :] == row_target[:, None]).astype(jnp.float32)
    )
    qq_weight = weight(masks[2], scores[2], row_norm) + weight(masks[2], scores[2], col_norm)
    dq_weight = (
        weight(masks[1], scores[1], row_doc_norm)
        + weight(masks[5], scores[1], col_norm)
        - (col_target[None, :] == row_global[:, None]).astype(jnp.float32)
    )
    dd_weight = weight(masks[3], scores[3], row_doc_norm) + weight(
        masks[3], scores[3], col_doc_norm
    )
    query_grad = (weighted(qd_weight, col_doc) + weighted(qq_weight, col_query)) * INV_TAU
    doc_grad = (weighted(dq_weight, col_query) + weighted(dd_weight, col_doc)) * INV_TAU
    query_part, doc_part = (
        lax.psum_scatter(query_grad, "inner", scatter_dimension=0, tiled=True),
        lax.psum_scatter(doc_grad, "inner", scatter_dimension=0, tiled=True),
    )
    grad_query = (
        query_part - unit_query * jnp.sum(unit_query * query_part, axis=1, keepdims=True)
    ) / query_len
    grad_doc = (doc_part - unit_doc * jnp.sum(unit_doc * doc_part, axis=1, keepdims=True)) / doc_len
    return (row_loss, grad_query, grad_doc)


def gather_kernel(
    depth, q_hbm, d_hbm, pos_hbm, qs_hbm, ds_hbm, out_ref,
    q_ref, d_ref, pos_ref, qs_ref, ds_ref, in_sem, buf, rows_all, unit_own, len_own, scol, ucol, srow, urow, lse_self, lse_pair, send_sem, recv_sem,
):
    f32, bf16 = jnp.float32, jnp.bfloat16
    rows = q_ref.shape[0]
    width = q_ref.shape[1]
    quarter = width // 4
    blk, inner = lax.axis_index("blk"), lax.axis_index("inner")
    z, y = blk // 2, blk % 2
    x, core = inner // 2, inner % 2
    me = blk * 4 + inner

    def place(zz, flip_a, flip_b):
        flip_y = flip_a * (1 - core) + flip_b * core
        flip_x = flip_a * core + flip_b * (1 - core)
        yy = y + flip_y * (1 - 2 * y)
        xx = x + flip_x * (1 - 2 * x)
        return zz * 2 + yy, xx * 2 + core

    def slot_of(zz, flip_a, flip_b):
        b, i = place(zz, flip_a, flip_b)
        return b * 4 + i

    peer_a = place(z, 1, 0)
    peer_b = place(z, 0, 1)
    peer_diag = place(z, 1, 1)
    peer_core = (blk, x * 2 + 1 - core)
    upper = z // (depth // 2)
    low = z * (1 - upper) + (depth - 1 - z) * upper

    def near(k):
        kth = k + jnp.minimum(jnp.maximum(k - low + 1, 0), 1)
        return kth * (1 - upper) + (depth - 1 - kth) * upper

    line = [near(k) for k in range(depth - 1)]

    barrier = pltpu.get_barrier_semaphore()
    peers = [(zz * 2 + y, inner) for zz in line] + [peer_a, peer_b, peer_diag, peer_core]
    for peer in peers:
        pl.semaphore_signal(barrier, inc=1, device_id=peer, device_id_type=pl.DeviceIdType.MESH)

    held = ((q_hbm, q_ref), (d_hbm, d_ref), (pos_hbm, pos_ref), (qs_hbm, qs_ref), (ds_hbm, ds_ref))
    loads = [pltpu.make_async_copy(a, b, in_sem.at[n]) for n, (a, b) in enumerate(held)]
    for load in loads:
        load.start()
    for load in loads:
        load.wait()
    unit_own[...] = jnp.zeros_like(unit_own)
    len_own[...] = jnp.ones_like(len_own)
    for ref, first in ((q_ref, 0), (d_ref, 16)):
        wide = ref[...].astype(f32)
        lengths = jnp.sqrt(jnp.sum(wide * wide, axis=1, keepdims=True) + EPS)
        unit_own[pl.ds(first, rows), :] = wide / lengths
        len_own[pl.ds(first, rows), :] = jnp.broadcast_to(lengths, (rows, 128))
    own = unit_own[...].astype(bf16)

    row = lax.broadcasted_iota(jnp.int32, (32, 128), 0)
    lane = lax.broadcasted_iota(jnp.int32, (32, 128), 1)
    source = jnp.zeros((32, 128), jnp.int32)
    key = jnp.zeros((32, 128), jnp.int32)
    for r in range(rows):
        source = jnp.where(row == r, qs_ref[r], source)
        source = jnp.where(row == 16 + r, ds_ref[r], source)
        key = jnp.where(row == r, pos_ref[r], key)
    key = jnp.where(row >= 16, me * rows + row - 16, key)
    kind = jnp.where(row >= 16, 0.25, 0.0).astype(f32)
    valid = (row % 16) < rows
    own_source = source.astype(f32)
    own_key = jnp.where(valid, key.astype(f32) + kind, -100.0)
    parts = (
        (source >> 5).astype(f32),
        (source & 31).astype(f32),
        (key >> 5).astype(f32),
        (key & 31).astype(f32) + kind,
    )

    def lanes(first):
        out = jnp.zeros((32, 128), f32)
        for k, part in enumerate(parts):
            out = jnp.where(lane == first + k, part, out)
        return out.astype(bf16)

    def select(shape, chosen):
        r = lax.broadcasted_iota(jnp.int32, shape, 0)
        c = lax.broadcasted_iota(jnp.int32, shape, 1)
        return chosen(r, c).astype(f32).astype(bf16)

    def mm(a, b):
        return jnp.dot(a, b, preferred_element_type=f32)

    def mmt(a, b):
        return lax.dot_general(a, b, (((1,), (1,)), ((), ())), preferred_element_type=f32)

    head = select((16, 32), lambda r, c: c == jnp.where(r < rows, r, r + 16 - rows))
    rest = [
        select((16, 32), lambda r, c, k=k: (r // 4 == k) & (c == 32 - rows + r % 4)) for k in range(4)
    ]
    mine = pl.ds(pl.multiple_of(me * 16, 16), 16)
    buf[mine, 0:width] = mm(head, own).astype(bf16)
    tail = mm(rest[0], own[:, 0:quarter])
    for k in range(1, 4):
        tail = tail + mm(rest[k], own[:, k * quarter : (k + 1) * quarter])
    buf[mine, width : width + quarter] = tail.astype(bf16)
    buf[mine, width + quarter :] = (mm(head, lanes(0)) + mm(rest[0], lanes(4))).astype(bf16)

    pl.semaphore_wait(barrier, len(peers))

    def copy(slot, sem, peer):
        piece = buf.at[pl.ds(pl.multiple_of(slot * 16, 16), 16)]
        return pltpu.make_async_remote_copy(
            src_ref=piece, dst_ref=piece, send_sem=send_sem.at[sem], recv_sem=recv_sem.at[slot],
            device_id=peer, device_id_type=pl.DeviceIdType.MESH,
        )

    def onward(k, flip_a, flip_b):
        slot = slot_of(z if k == 0 else line[k - 1], flip_a, flip_b)
        out = []
        if not flip_a and not flip_b:
            if k == 0:
                for n, zz in enumerate(line):
                    out.append(copy(slot, n, (zz * 2 + y, inner)))
            out.append(copy(slot, depth + k, peer_a))
            out.append(copy(slot, 2 * depth + k, peer_b))
            out.append(copy(slot, 3 * depth + k, peer_diag))
        out.append(copy(slot, (4 + 2 * flip_b + flip_a) * depth + k, peer_core))
        return slot, out

    def arrive(slot):
        copy(slot, 0, peer_core).wait_recv()

    order = sorted((k + (flip_a + flip_b), flip_a + flip_b, k, flip_a, flip_b)
                   for k in range(depth) for flip_a in (0, 1) for flip_b in (0, 1))
    started = []
    for _, hops, k, flip_a, flip_b in order:
        slot, copies = onward(k, flip_a, flip_b)
        if k or hops:
            arrive(slot)
        for one in copies:
            one.start()
        started += copies

    def from_core(zz, carry):
        for fb in (0, 1):
            for fa in (0, 1):
                s = slot_of(zz, fa, fb)
                arrive(s + 1 - 2 * core)
        return carry

    lax.fori_loop(0, depth, from_core, 0)

    count = 2 * rows * buf.shape[0] // 16
    heads = buf.shape[0]
    tails = count - heads
    rows_all[0:heads, :] = buf[:, 0:width]
    left = buf[:, width : width + quarter]
    meta = buf[:, width + quarter :]
    picks = [
        select((tails, heads), lambda r, c, k=k: c == r // 4 * 16 + k * 4 + r % 4) for k in range(4)
    ]
    for k in range(4):
        rows_all[heads:count, k * quarter : (k + 1) * quarter] = mm(picks[k], left).astype(bf16)
    rows_all[count:, :] = own
    meta_tail = mm(picks[0], meta).astype(bf16)

    def reader(first, axis, shape):
        pos = lax.broadcasted_iota(jnp.int32, shape, axis)
        return jnp.where(pos == first, 32.0, jnp.where(pos == first + 1, 1.0, 0.0)).astype(bf16)

    for ref, first in ((scol, 0), (ucol, 2)):
        ref[0:heads, :] = mm(meta, reader(first, 0, (128, 128)))
        ref[heads:, :] = mm(meta_tail, reader(first + 4, 0, (128, 128)))
    for ref, first in ((srow, 0), (urow, 2)):
        ref[:, 0:heads] = mmt(reader(first, 1, (8, 128)), meta)
        ref[:, heads:] = mmt(reader(first + 4, 1, (8, 128)), meta_tail)
    s_row, u_row = srow[0:1, :], urow[0:1, :]
    everything = mmt(rows_all[...], rows_all[0:count, :]) * INV_TAU
    apart = u_row - ucol[:, 0:1]
    allowed = (apart == 0.25) | ((s_row != scol[:, 0:1]) & (apart != -0.25))
    scores = jnp.where(allowed, everything[0:count, :], NEG)
    peak = jnp.max(scores, axis=1, keepdims=True)
    total = jnp.sum(jnp.exp(scores - peak), axis=1, keepdims=True)
    lse = jnp.where(peak > 0.5 * NEG, peak + jnp.log(total), NEG)
    first = jnp.sum(jnp.where(apart == 0.0, lse, 0.0), axis=0, keepdims=True)
    second = jnp.sum(jnp.where(jnp.abs(apart) == 0.25, lse, 0.0), axis=0, keepdims=True)
    norm_row = jnp.maximum(first, second) + jnp.log(1.0 + jnp.exp(-jnp.abs(first - second)))

    scores = everything[count:, :]
    apart = u_row - own_key[:, 0:1]
    hit = jnp.abs(apart) == 0.25
    norm_own = jnp.sum(jnp.where(apart == 0.0, norm_row, 0.0), axis=1, keepdims=True)
    loss = norm_own - jnp.sum(jnp.where(hit, scores, 0.0), axis=1, keepdims=True)
    out_ref[:, width:] = jnp.broadcast_to(loss, (32, 128))
    from_own = jnp.exp(scores - norm_own)
    apart_source = (s_row != own_source[:, 0:1]) & (own_key[:, 0:1] >= 0.0)
    weights = jnp.where(
        hit, from_own - 1.0, jnp.where(apart_source, from_own + jnp.exp(scores - norm_row), 0.0)
    )
    grads = mm(weights.astype(bf16), rows_all[0:count, :]) * INV_TAU
    unit = unit_own[...]
    grads = (grads - unit * jnp.sum(unit * grads, axis=1, keepdims=True)) / len_own[:, 0:1]
    out_ref[:, 0:width] = grads

    for one in started:
        one.wait_send()


def whole_batch(depth, query_emb, doc_emb, positive, query_source, doc_source):
    rows, width = query_emb.shape
    devices = lax.axis_size("blk") * lax.axis_size("inner")
    count = 2 * rows * devices
    vmem = pl.BlockSpec(memory_space=pltpu.VMEM)
    f32 = jnp.float32
    out = pl.pallas_call(
        functools.partial(gather_kernel, depth),
        out_shape=jax.ShapeDtypeStruct((32, width + 128), f32),
        in_specs=[pl.BlockSpec(memory_space=pltpu.HBM)] * 5,
        out_specs=vmem,
        scratch_shapes=[
            pltpu.VMEM((rows, width), jnp.bfloat16),
            pltpu.VMEM((rows, width), jnp.bfloat16),
            pltpu.SMEM((rows,), jnp.int32),
            pltpu.SMEM((rows,), jnp.int32),
            pltpu.SMEM((rows,), jnp.int32),
            pltpu.SemaphoreType.DMA((5,)),
            pltpu.VMEM((devices * 16, width + width // 4 + 128), jnp.bfloat16),
            pltpu.VMEM((count + 32, width), jnp.bfloat16),
            pltpu.VMEM((32, width), f32),
            pltpu.VMEM((32, 128), f32),
            pltpu.VMEM((count, 128), f32),
            pltpu.VMEM((count, 128), f32),
            pltpu.VMEM((8, count), f32),
            pltpu.VMEM((8, count), f32),
            pltpu.VMEM((8, count), f32),
            pltpu.VMEM((8, count), f32),
            pltpu.SemaphoreType.DMA((8 * depth,)),
            pltpu.SemaphoreType.DMA((devices,)),
        ],
        compiler_params=pltpu.CompilerParams(
            collective_id=0, has_side_effects=True, vmem_limit_bytes=56 * 1024 * 1024
        ),
    )(query_emb, doc_emb, positive, query_source, doc_source)
    return (out[:rows, width], out[:rows, :width], out[16 : 16 + rows, :width])


def solution(mesh):
    small = mesh.shape["inner"] == 4 and mesh.shape["blk"] == 8
    body = functools.partial(whole_batch, mesh.shape["blk"] // 2) if small else shards
    placed = (
        P(("blk", "inner"), None),
        P(("blk", "inner"), None),
        P(("blk", "inner")),
        P(("blk", "inner")),
        P(("blk", "inner")),
    )
    return jax.shard_map(
        body,
        mesh=mesh,
        in_specs=placed,
        out_specs=(P(("blk", "inner")), P(("blk", "inner"), None), P(("blk", "inner"), None)),
        check_vma=False,
    )
```

```python
import functools

import jax
import jax.numpy as jnp
from jax import lax
from jax.experimental import pallas as pl
from jax.experimental.pallas import tpu as pltpu
from jax.sharding import PartitionSpec as P

EPS = 1e-06
INV_TAU = 100.0
NEG = -1e30


def joined_2(value, axis, join):
    pieces = jax.tree.map(lambda part: lax.all_gather(part, axis), value)
    head = jax.tree.map(lambda part: part[0], pieces)
    tail = jax.tree.map(lambda part: part[1:], pieces)
    so_far, _ = lax.scan(lambda so_far, piece: (join(so_far, piece), None), head, tail)
    return so_far


def unit_rows(values):
    widened = values.astype(jnp.float32)
    lengths = jnp.sqrt(jnp.sum(widened * widened, axis=1, keepdims=True) + EPS)
    return (widened / lengths, lengths)


def scaled_gram(left_rows, right_rows):
    return (
        lax.dot_general(
            left_rows, right_rows, (((1,), (1,)), ((), ())), preferred_element_type=jnp.float32
        )
        * INV_TAU
    )


def pair_masks(row_info, col_info):
    row_qsource, row_dsource, row_target, row_global = row_info
    col_qsource, col_dsource, col_target, col_global = col_info
    mask_qd = (col_global[None, :] == row_target[:, None]) | (
        col_dsource[None, :] != row_qsource[:, None]
    )
    mask_dq = (col_target[None, :] != row_global[:, None]) & (
        col_qsource[None, :] != row_dsource[:, None]
    )
    mask_qq = col_qsource[None, :] != row_qsource[:, None]
    mask_dd = col_dsource[None, :] != row_dsource[:, None]
    twin_dq = (row_target[:, None] != col_global[None, :]) & (
        row_qsource[:, None] != col_dsource[None, :]
    )
    twin_qd = (row_global[:, None] == col_target[None, :]) | (
        row_dsource[:, None] != col_qsource[None, :]
    )
    return (mask_qd, mask_dq, mask_qq, mask_dd, twin_dq, twin_qd)


def masked_terms(scores_list, masks_list):
    peak = jnp.max(jnp.where(masks_list[0], scores_list[0], NEG), axis=1)
    for scores, masked in zip(scores_list[1:], masks_list[1:]):
        peak = jnp.maximum(peak, jnp.max(jnp.where(masked, scores, NEG), axis=1))
    totals = jnp.zeros(peak.shape, jnp.float32)
    for scores, masked in zip(scores_list, masks_list):
        totals = totals + jnp.sum(jnp.exp(jnp.where(masked, scores - peak[:, None], NEG)), axis=1)
    return (peak, totals)


def joined(former, latter):
    peak = jnp.maximum(former[0], latter[0])
    return (peak, former[1] * jnp.exp(former[0] - peak) + latter[1] * jnp.exp(latter[0] - peak))


def merge_stats(former, latter):
    query_pair = joined((former[0], former[1]), (latter[0], latter[1]))
    doc_pair = joined((former[2], former[3]), (latter[2], latter[3]))
    return (query_pair[0], query_pair[1], doc_pair[0], doc_pair[1], former[4] + latter[4])


def column_global(offset, amount, rows_dev, inner_count, inner_pos):
    flat = offset + jnp.arange(amount, dtype=jnp.int32)
    return flat // rows_dev * (inner_count * rows_dev) + inner_pos * rows_dev + flat % rows_dev


def weight(masked, scores, norms):
    return jnp.exp(jnp.where(masked, scores - norms, NEG))


def weighted(weights, right_rows):
    return jnp.dot(weights.astype(jnp.bfloat16), right_rows, preferred_element_type=jnp.float32)


def shards(query_emb, doc_emb, positive, query_source, doc_source):
    rows_dev = query_emb.shape[0]
    inner_count = lax.axis_size("inner")
    inner_pos = lax.axis_index("inner")
    blk_pos = lax.axis_index("blk")
    group_base = blk_pos * inner_count * rows_dev
    unit_query, query_len = unit_rows(query_emb)
    unit_doc, doc_len = unit_rows(doc_emb)
    query_half = unit_query.astype(jnp.bfloat16)
    doc_half = unit_doc.astype(jnp.bfloat16)
    row_query, row_doc, row_qsource, row_dsource, row_target = (
        lax.all_gather(query_half, "inner", axis=0, tiled=True),
        lax.all_gather(doc_half, "inner", axis=0, tiled=True),
        lax.all_gather(query_source, "inner", axis=0, tiled=True),
        lax.all_gather(doc_source, "inner", axis=0, tiled=True),
        lax.all_gather(positive, "inner", axis=0, tiled=True),
    )
    row_global = group_base + jnp.arange(row_query.shape[0], dtype=jnp.int32)
    own_start = inner_pos * rows_dev

    def col_index(offset, amount):
        return column_global(offset, amount, rows_dev, inner_count, inner_pos)

    row_count = row_query.shape[0]
    row_info = (row_qsource, row_dsource, row_target, row_global)

    def tile(pieces, offset):
        col_query, col_doc, col_qsource, col_dsource, col_target = pieces
        col_global = col_index(offset, col_query.shape[0])
        scores = (
            scaled_gram(row_query, col_doc),
            scaled_gram(row_doc, col_query),
            scaled_gram(row_query, col_query),
            scaled_gram(row_doc, col_doc),
        )
        masks = pair_masks(row_info, (col_qsource, col_dsource, col_target, col_global))
        return (col_global, scores, masks)

    empty_peak = jnp.full((row_count,), NEG, jnp.float32)
    empty_sum = jnp.zeros((row_count,), jnp.float32)
    start_stats = (empty_peak, empty_sum, empty_peak, empty_sum, empty_sum)
    columns = (
        lax.all_gather(query_half, "blk", axis=0, tiled=True),
        lax.all_gather(doc_half, "blk", axis=0, tiled=True),
        lax.all_gather(query_source, "blk", axis=0, tiled=True),
        lax.all_gather(doc_source, "blk", axis=0, tiled=True),
        lax.all_gather(positive, "blk", axis=0, tiled=True),
    )
    col_global, scores, masks = tile(columns, 0)
    query_side = masked_terms([scores[0], scores[2]], [masks[0], masks[2]])
    doc_side = masked_terms([scores[1], scores[3]], [masks[1], masks[3]])
    hit = jnp.sum(jnp.where(col_global[None, :] == row_target[:, None], scores[0], 0.0), axis=1)
    stats = merge_stats(start_stats, (query_side[0], query_side[1], doc_side[0], doc_side[1], hit))
    stats = joined_2(stats, "inner", merge_stats)
    query_lse = stats[0] + jnp.log(stats[1])
    doc_lse = stats[2] + jnp.log(stats[3])
    own_doc_lse = lax.dynamic_slice_in_dim(doc_lse, own_start, rows_dev, 0)
    doc_lse_all, target_all = (
        lax.all_gather(own_doc_lse, ("blk", "inner"), axis=0, tiled=True),
        lax.all_gather(positive, ("blk", "inner"), axis=0, tiled=True),
    )
    own_query_lse = lax.dynamic_slice_in_dim(query_lse, own_start, rows_dev, 0)
    own_hit = lax.dynamic_slice_in_dim(stats[4], own_start, rows_dev, 0)
    own_norm = jnp.logaddexp(own_query_lse, jnp.take(doc_lse_all, positive))
    row_loss = own_norm - own_hit
    norm_all = lax.all_gather(own_norm, ("blk", "inner"), axis=0, tiled=True)
    pairs = norm_all.shape[0]
    inverse = jnp.zeros((pairs,), jnp.int32).at[target_all].set(jnp.arange(pairs, dtype=jnp.int32))
    doc_norm_all = jnp.take(norm_all, inverse)
    row_norm = jnp.take(norm_all, row_global)[:, None]
    row_doc_norm = jnp.take(doc_norm_all, row_global)[:, None]
    col_global, scores, masks = tile(columns, 0)
    col_query = columns[0]
    col_doc = columns[1]
    col_target = columns[4]
    col_norm = jnp.take(norm_all, col_global)[None, :]
    col_doc_norm = jnp.take(doc_norm_all, col_global)[None, :]
    qd_weight = (
        weight(masks[0], scores[0], row_norm)
        + weight(masks[4], scores[0], col_doc_norm)
        - (col_global[None, :] == row_target[:, None]).astype(jnp.float32)
    )
    qq_weight = weight(masks[2], scores[2], row_norm) + weight(masks[2], scores[2], col_norm)
    dq_weight = (
        weight(masks[1], scores[1], row_doc_norm)
        + weight(masks[5], scores[1], col_norm)
        - (col_target[None, :] == row_global[:, None]).astype(jnp.float32)
    )
    dd_weight = weight(masks[3], scores[3], row_doc_norm) + weight(
        masks[3], scores[3], col_doc_norm
    )
    query_grad = (weighted(qd_weight, col_doc) + weighted(qq_weight, col_query)) * INV_TAU
    doc_grad = (weighted(dq_weight, col_query) + weighted(dd_weight, col_doc)) * INV_TAU
    query_part, doc_part = (
        lax.psum_scatter(query_grad, "inner", scatter_dimension=0, tiled=True),
        lax.psum_scatter(doc_grad, "inner", scatter_dimension=0, tiled=True),
    )
    grad_query = (
        query_part - unit_query * jnp.sum(unit_query * query_part, axis=1, keepdims=True)
    ) / query_len
    grad_doc = (doc_part - unit_doc * jnp.sum(unit_doc * doc_part, axis=1, keepdims=True)) / doc_len
    return (row_loss, grad_query, grad_doc)


def gather_kernel(
    depth, q_hbm, d_hbm, pos_hbm, qs_hbm, ds_hbm, out_ref,
    q_ref, d_ref, pos_ref, qs_ref, ds_ref, in_sem, buf, rows_all, unit_own, len_own, scol, ucol, srow, urow, lse_self, lse_pair, send_sem, recv_sem,
):
    f32, bf16 = jnp.float32, jnp.bfloat16
    rows = q_ref.shape[0]
    width = q_ref.shape[1]
    quarter = width // 4
    blk, inner = lax.axis_index("blk"), lax.axis_index("inner")
    z, y = blk // 2, blk % 2
    x, core = inner // 2, inner % 2
    me = blk * 4 + inner

    def place(zz, flip_a, flip_b):
        flip_y = flip_a * (1 - core) + flip_b * core
        flip_x = flip_a * core + flip_b * (1 - core)
        yy = y + flip_y * (1 - 2 * y)
        xx = x + flip_x * (1 - 2 * x)
        return zz * 2 + yy, xx * 2 + core

    def slot_of(zz, flip_a, flip_b):
        b, i = place(zz, flip_a, flip_b)
        return b * 4 + i

    peer_a = place(z, 1, 0)
    peer_b = place(z, 0, 1)
    peer_diag = place(z, 1, 1)
    peer_core = (blk, x * 2 + 1 - core)
    upper = z // (depth // 2)
    low = z * (1 - upper) + (depth - 1 - z) * upper

    def near(k):
        kth = k + jnp.minimum(jnp.maximum(k - low + 1, 0), 1)
        return kth * (1 - upper) + (depth - 1 - kth) * upper

    line = [near(k) for k in range(depth - 1)]

    barrier = pltpu.get_barrier_semaphore()
    peers = [(zz * 2 + y, inner) for zz in line] + [peer_a, peer_b, peer_diag, peer_core]
    for peer in peers:
        pl.semaphore_signal(barrier, inc=1, device_id=peer, device_id_type=pl.DeviceIdType.MESH)

    held = ((q_hbm, q_ref), (d_hbm, d_ref), (pos_hbm, pos_ref), (qs_hbm, qs_ref), (ds_hbm, ds_ref))
    loads = [pltpu.make_async_copy(a, b, in_sem.at[n]) for n, (a, b) in enumerate(held)]
    for load in loads:
        load.start()
    for load in loads:
        load.wait()
    unit_own[...] = jnp.zeros_like(unit_own)
    len_own[...] = jnp.ones_like(len_own)
    for ref, first in ((q_ref, 0), (d_ref, 16)):
        wide = ref[...].astype(f32)
        lengths = jnp.sqrt(jnp.sum(wide * wide, axis=1, keepdims=True) + EPS)
        unit_own[pl.ds(first, rows), :] = wide / lengths
        len_own[pl.ds(first, rows), :] = jnp.broadcast_to(lengths, (rows, 128))
    own = unit_own[...].astype(bf16)

    row = lax.broadcasted_iota(jnp.int32, (32, 128), 0)
    lane = lax.broadcasted_iota(jnp.int32, (32, 128), 1)
    source = jnp.zeros((32, 128), jnp.int32)
    key = jnp.zeros((32, 128), jnp.int32)
    for r in range(rows):
        source = jnp.where(row == r, qs_ref[r], source)
        source = jnp.where(row == 16 + r, ds_ref[r], source)
        key = jnp.where(row == r, pos_ref[r], key)
    key = jnp.where(row >= 16, me * rows + row - 16, key)
    kind = jnp.where(row >= 16, 0.25, 0.0).astype(f32)
    valid = (row % 16) < rows
    own_source = source.astype(f32)
    own_key = jnp.where(valid, key.astype(f32) + kind, -100.0)
    parts = (
        (source >> 5).astype(f32),
        (source & 31).astype(f32),
        (key >> 5).astype(f32),
        (key & 31).astype(f32) + kind,
    )

    def lanes(first):
        out = jnp.zeros((32, 128), f32)
        for k, part in enumerate(parts):
            out = jnp.where(lane == first + k, part, out)
        return out.astype(bf16)

    def select(shape, chosen):
        r = lax.broadcasted_iota(jnp.int32, shape, 0)
        c = lax.broadcasted_iota(jnp.int32, shape, 1)
        return chosen(r, c).astype(f32).astype(bf16)

    def mm(a, b):
        return jnp.dot(a, b, preferred_element_type=f32)

    def mmt(a, b):
        return lax.dot_general(a, b, (((1,), (1,)), ((), ())), preferred_element_type=f32)

    head = select((16, 32), lambda r, c: c == jnp.where(r < rows, r, r + 16 - rows))
    rest = [
        select((16, 32), lambda r, c, k=k: (r // 4 == k) & (c == 32 - rows + r % 4)) for k in range(4)
    ]
    mine = pl.ds(pl.multiple_of(me * 16, 16), 16)
    buf[mine, 0:width] = mm(head, own).astype(bf16)
    tail = mm(rest[0], own[:, 0:quarter])
    for k in range(1, 4):
        tail = tail + mm(rest[k], own[:, k * quarter : (k + 1) * quarter])
    buf[mine, width : width + quarter] = tail.astype(bf16)
    buf[mine, width + quarter :] = (mm(head, lanes(0)) + mm(rest[0], lanes(4))).astype(bf16)

    pl.semaphore_wait(barrier, len(peers))

    def copy(slot, sem, peer):
        piece = buf.at[pl.ds(pl.multiple_of(slot * 16, 16), 16)]
        return pltpu.make_async_remote_copy(
            src_ref=piece, dst_ref=piece, send_sem=send_sem.at[sem], recv_sem=recv_sem.at[slot],
            device_id=peer, device_id_type=pl.DeviceIdType.MESH,
        )

    def onward(k, flip_a, flip_b):
        slot = slot_of(z if k == 0 else line[k - 1], flip_a, flip_b)
        out = []
        if not flip_a and not flip_b:
            if k == 0:
                for n, zz in enumerate(line):
                    out.append(copy(slot, n, (zz * 2 + y, inner)))
            out.append(copy(slot, depth + k, peer_a))
            out.append(copy(slot, 2 * depth + k, peer_b))
            out.append(copy(slot, 3 * depth + k, peer_diag))
        out.append(copy(slot, (4 + 2 * flip_b + flip_a) * depth + k, peer_core))
        return slot, out

    def arrive(slot):
        copy(slot, 0, peer_core).wait_recv()

    order = sorted((k + (flip_a + flip_b), flip_a + flip_b, k, flip_a, flip_b)
                   for k in range(depth) for flip_a in (0, 1) for flip_b in (0, 1))
    started = []
    for _, hops, k, flip_a, flip_b in order:
        slot, copies = onward(k, flip_a, flip_b)
        if k or hops:
            arrive(slot)
        for one in copies:
            one.start()
        started += copies

    def from_core(zz, carry):
        for fb in (0, 1):
            for fa in (0, 1):
                s = slot_of(zz, fa, fb)
                arrive(s + 1 - 2 * core)
        return carry

    def place_rows(pair, which):
        at = pl.ds(pl.multiple_of((2 * pair + which) * 16, 16), 16)
        rows_all[at, :] = buf[at, 0:width]
        return which

    lax.fori_loop(0, buf.shape[0] // 32, place_rows, core)
    lax.fori_loop(0, depth, from_core, 0)
    lax.fori_loop(0, buf.shape[0] // 32, place_rows, 1 - core)

    count = 2 * rows * buf.shape[0] // 16
    heads = buf.shape[0]
    tails = count - heads
    left = buf[:, width : width + quarter]
    meta = buf[:, width + quarter :]
    picks = [
        select((tails, heads), lambda r, c, k=k: c == r // 4 * 16 + k * 4 + r % 4) for k in range(4)
    ]
    for k in range(4):
        rows_all[heads:count, k * quarter : (k + 1) * quarter] = mm(picks[k], left).astype(bf16)
    rows_all[count:, :] = own
    meta_tail = mm(picks[0], meta).astype(bf16)

    def reader(first, axis, shape):
        pos = lax.broadcasted_iota(jnp.int32, shape, axis)
        return jnp.where(pos == first, 32.0, jnp.where(pos == first + 1, 1.0, 0.0)).astype(bf16)

    for ref, first in ((scol, 0), (ucol, 2)):
        ref[0:heads, :] = mm(meta, reader(first, 0, (128, 128)))
        ref[heads:, :] = mm(meta_tail, reader(first + 4, 0, (128, 128)))
    for ref, first in ((srow, 0), (urow, 2)):
        ref[:, 0:heads] = mmt(reader(first, 1, (8, 128)), meta)
        ref[:, heads:] = mmt(reader(first + 4, 1, (8, 128)), meta_tail)
    s_row, u_row = srow[0:1, :], urow[0:1, :]
    everything = mmt(rows_all[...], rows_all[0:count, :]) * INV_TAU
    apart = u_row - ucol[:, 0:1]
    allowed = (apart == 0.25) | ((s_row != scol[:, 0:1]) & (apart != -0.25))
    scores = jnp.where(allowed, everything[0:count, :], NEG)
    peak = jnp.max(scores, axis=1, keepdims=True)
    total = jnp.sum(jnp.exp(scores - peak), axis=1, keepdims=True)
    lse = jnp.where(peak > 0.5 * NEG, peak + jnp.log(total), NEG)
    first = jnp.sum(jnp.where(apart == 0.0, lse, 0.0), axis=0, keepdims=True)
    second = jnp.sum(jnp.where(jnp.abs(apart) == 0.25, lse, 0.0), axis=0, keepdims=True)
    norm_row = jnp.maximum(first, second) + jnp.log(1.0 + jnp.exp(-jnp.abs(first - second)))

    scores = everything[count:, :]
    apart = u_row - own_key[:, 0:1]
    hit = jnp.abs(apart) == 0.25
    norm_own = jnp.sum(jnp.where(apart == 0.0, norm_row, 0.0), axis=1, keepdims=True)
    loss = norm_own - jnp.sum(jnp.where(hit, scores, 0.0), axis=1, keepdims=True)
    out_ref[:, width:] = jnp.broadcast_to(loss, (32, 128))
    from_own = jnp.exp(scores - norm_own)
    apart_source = (s_row != own_source[:, 0:1]) & (own_key[:, 0:1] >= 0.0)
    weights = jnp.where(
        hit, from_own - 1.0, jnp.where(apart_source, from_own + jnp.exp(scores - norm_row), 0.0)
    )
    grads = mm(weights.astype(bf16), rows_all[0:count, :]) * INV_TAU
    unit = unit_own[...]
    grads = (grads - unit * jnp.sum(unit * grads, axis=1, keepdims=True)) / len_own[:, 0:1]
    out_ref[:, 0:width] = grads

    for one in started:
        one.wait_send()


def whole_batch(depth, query_emb, doc_emb, positive, query_source, doc_source):
    rows, width = query_emb.shape
    devices = lax.axis_size("blk") * lax.axis_size("inner")
    count = 2 * rows * devices
    vmem = pl.BlockSpec(memory_space=pltpu.VMEM)
    f32 = jnp.float32
    out = pl.pallas_call(
        functools.partial(gather_kernel, depth),
        out_shape=jax.ShapeDtypeStruct((32, width + 128), f32),
        in_specs=[pl.BlockSpec(memory_space=pltpu.HBM)] * 5,
        out_specs=vmem,
        scratch_shapes=[
            pltpu.VMEM((rows, width), jnp.bfloat16),
            pltpu.VMEM((rows, width), jnp.bfloat16),
            pltpu.SMEM((rows,), jnp.int32),
            pltpu.SMEM((rows,), jnp.int32),
            pltpu.SMEM((rows,), jnp.int32),
            pltpu.SemaphoreType.DMA((5,)),
            pltpu.VMEM((devices * 16, width + width // 4 + 128), jnp.bfloat16),
            pltpu.VMEM((count + 32, width), jnp.bfloat16),
            pltpu.VMEM((32, width), f32),
            pltpu.VMEM((32, 128), f32),
            pltpu.VMEM((count, 128), f32),
            pltpu.VMEM((count, 128), f32),
            pltpu.VMEM((8, count), f32),
            pltpu.VMEM((8, count), f32),
            pltpu.VMEM((8, count), f32),
            pltpu.VMEM((8, count), f32),
            pltpu.SemaphoreType.DMA((8 * depth,)),
            pltpu.SemaphoreType.DMA((devices,)),
        ],
        compiler_params=pltpu.CompilerParams(
            collective_id=0, has_side_effects=True, vmem_limit_bytes=56 * 1024 * 1024
        ),
    )(query_emb, doc_emb, positive, query_source, doc_source)
    return (out[:rows, width], out[:rows, :width], out[16 : 16 + rows, :width])


def solution(mesh):
    small = mesh.shape["inner"] == 4 and mesh.shape["blk"] == 8
    body = functools.partial(whole_batch, mesh.shape["blk"] // 2) if small else shards
    placed = (
        P(("blk", "inner"), None),
        P(("blk", "inner"), None),
        P(("blk", "inner")),
        P(("blk", "inner")),
        P(("blk", "inner")),
    )
    return jax.shard_map(
        body,
        mesh=mesh,
        in_specs=placed,
        out_specs=(P(("blk", "inner")), P(("blk", "inner"), None), P(("blk", "inner"), None)),
        check_vma=False,
    )
```
